512 devices in a mesh: pipe: 16 (over x, y_hi, core), tensor: 32 (over y_lo, z).
Axes of the slice: x: 4, y: 4 (y_hi: 2, y_lo: 2; y = y_hi * 2 + y_lo), z: 16, core: 2. Of those that a mesh axis runs over, the one named last changes fastest.
Arguments:
- ssm_inputs: bfloat16 [4096, 8192], P('pipe', 'tensor'), may hold values from -6 to 6
- step_decay: float32 [128, 4096], P('tensor', 'pipe'), may hold values from 0 to 1
- state_inputs: bfloat16 [8, 4096, 128], P(None, 'pipe'), may hold values from -1.5 to 1.5
- state_readout: bfloat16 [8, 4096, 128], P(None, 'pipe'), may hold values from -6 to 6
- skip_gain: float32 [128], P('tensor'), may hold values from 0.5 to 2
- norm_gain: float32 [8192], P('tensor'), may hold values from 0.5 to 1.5
- new_keys: bfloat16 [8, 4096, 128], P(None, 'pipe'), may hold values from -200 to 200
- new_values: bfloat16 [8, 4096, 128], P(None, 'pipe'), may hold values from -6 to 6
- cache_keys: bfloat16 [8, 2048, 128], P(None, 'pipe'), may hold values from -6 to 6
- cache_values: bfloat16 [8, 2048, 128], P(None, 'pipe'), may hold values from -6 to 6
- cache_len: int32 [16], P('pipe'), may hold values from 1 to 128, 1088 in all
- out_weight: bfloat16 [8192, 4096], P('tensor'), may hold values from -0.0625 to 0.0625
Outputs:
- mixed: bfloat16 [4096, 4096], P(('pipe', 'tensor'))
The draws below stay inside these ranges and needn't reach their ends.
All inputs are finite; a program needn't handle non-finite values. No bound on the sum of `cache_len` on one device may be relied on, other than what follows from the above.
Results may differ from the reference program's by a relative error of at most 0.03.
Values may be sent and summed in bfloat16 or wider, within the bound.
No kernel may reach another device: no remote copies, remote signals or barrier semaphores. Data moves between devices by JAX's collectives and lax.ppermute only.
A program may use at most 64 MiB of HBM per device.

```python
import math
import jax
import jax.numpy as jnp
import numpy as np
from jax import lax

TOKENS_PER_SLICE = 256
CACHE = 128
MH = 128
P_SIZE = 64
STATE = 128
GROUPS = 8
ATT_HEADS = 64
KV = 8
HD = 128
DOUT = 4096
STREAM_ITEMS = 4096
N_PIPE = 16


def draw_step_decay(key, part):
    key = jax.random.fold_in(key, 11)
    stochastic_seeds = jax.random.split(key, 6)
    lagging_fraction = 0.5
    is_slow = jax.random.uniform(stochastic_seeds[0], (MH,)) < lagging_fraction
    slow = jnp.exp(jax.random.uniform(stochastic_seeds[1], (MH,), minval=math.log(0.2 / STREAM_ITEMS), maxval=math.log(1.0 / STREAM_ITEMS)))
    fast = jnp.exp(jax.random.uniform(stochastic_seeds[2], (MH,), minval=math.log(1.0 / 50.0), maxval=math.log(1.0 / 30.0)))
    descent_stepsize = jnp.where(is_slow, slow, fast)
    magnitude_multiplier = jax.random.uniform(stochastic_seeds[3], (MH, STREAM_ITEMS), minval=0.5, maxval=1.5)
    cluster_batches = jax.random.uniform(stochastic_seeds[4], (STREAM_ITEMS,)) < 2.0 / STREAM_ITEMS
    objective_measure = jax.random.uniform(stochastic_seeds[5], (MH, STREAM_ITEMS), minval=0.22, maxval=0.69)
    return (descent_stepsize[:, None] * magnitude_multiplier + jnp.where(cluster_batches[None, :], objective_measure, 0.0)).astype(jnp.float32)


def draw_new_keys(key, part):
    key = jax.random.fold_in(key, 17)
    stochastic_seeds = jax.random.split(key, 1)
    base = jnp.clip(jax.random.normal(stochastic_seeds[0], (KV, STREAM_ITEMS, HD), jnp.float32), -6.0, 6.0)
    return base.astype(jnp.bfloat16)


def steps_of(own_key, shape, shards, smallest, high):
    level = 1.0
    for dim, blocks in shards:
        steps = jax.random.uniform(jax.random.fold_in(jax.random.fold_in(own_key, 6), dim), (blocks,), jnp.float32, smallest / len(shards), high / len(shards))
        level = level * jnp.repeat(jnp.exp(steps), shape[dim] // blocks).reshape((-1,) + (1,) * (len(shape) - 1 - dim))
    return level


def split_up(number_of, total, limit, skew):
    loads = [(1 << 20) // math.isqrt(rank ** skew) + 1 for rank in range(2, number_of + 1)]
    spare, holding = total - limit - (number_of - 1), [1] * (number_of - 1)
    while spare > 0:
        free = [i for i in range(number_of - 1) if holding[i] < limit]
        pool, remaining = sum([loads[i] for i in free]), spare
        for i in free:
            extra = min(limit - holding[i], max(1, remaining * loads[i] // pool), spare)
            holding[i] = holding[i] + extra
            spare = spare - extra
    return np.array([limit] + holding)


def uneven_parts(key, amount, total, limit, lean):
    if amount == 2:
        one = jax.random.randint(key, (), max(1, total - limit), min(limit, total - 1) + 1)
        return jnp.stack([one, total - one])
    lengths = jnp.asarray(split_up(amount, total, limit, lean), jnp.int32)
    couples = (amount - 1) // 2
    source_of, sink = lengths[1:1 + 2 * couples:2], lengths[2:2 + 2 * couples:2]
    room = jnp.minimum(source_of - 1, limit - sink)
    shifted = jax.random.randint(jax.random.fold_in(key, 1), (couples,), 0, 1 << 20) % (room + 1)
    lengths = lengths.at[1:1 + 2 * couples:2].set(source_of - shifted).at[2:2 + 2 * couples:2].set(sink + shifted)
    return lengths[jax.random.permutation(jax.random.fold_in(key, 2), amount)]


def scatter_about(rng, shape, width, most, cuts=(), dtype=jnp.bfloat16):
    entries = width * jax.random.normal(rng, shape, jnp.float32)
    if cuts:
        entries = entries * steps_of(rng, shape, cuts, -0.22, 0.18)
    return jnp.clip(entries, -most, most).astype(dtype)


def setup_inputs(seed: int = 0) -> dict:
    arg_keys = jax.random.split(jax.random.key(seed), 13)
    ssm_inputs = scatter_about(arg_keys[0], (STREAM_ITEMS, MH * P_SIZE), 1.0, 6.0, ((0, 16), (1, 32)))
    step_decay = draw_step_decay(jax.random.fold_in(arg_keys[12], 71), 0)
    state_inputs = scatter_about(arg_keys[2], (GROUPS, STREAM_ITEMS, STATE), 0.1, 1.5, ((1, 16),))
    state_readout = scatter_about(arg_keys[3], (GROUPS, STREAM_ITEMS, STATE), 1.0, 6.0, ((1, 16),))
    skip_gain = jnp.clip(0.5 + 1.5 * jax.random.uniform(arg_keys[4], (MH,), jnp.float32) ** steps_of(arg_keys[4], (MH,), ((0, 32),), -0.2, 0.2), 0.5, 2.0)
    norm_gain = jnp.clip(1.0 + 0.1 * jax.random.normal(arg_keys[5], (MH * P_SIZE,), jnp.float32), 0.5, 1.5)
    new_keys = draw_new_keys(jax.random.fold_in(arg_keys[12], 71), 0)
    new_values = scatter_about(arg_keys[7], (KV, STREAM_ITEMS, HD), 1.0, 6.0, ((1, 16),))
    cache_keys = scatter_about(arg_keys[8], (KV, CACHE * N_PIPE, HD), 1.0, 6.0, ((1, 16),))
    cache_values = scatter_about(arg_keys[9], (KV, CACHE * N_PIPE, HD), 1.0, 6.0, ((1, 16),))
    cache_len = uneven_parts(arg_keys[10], N_PIPE, N_PIPE * CACHE // 2 + CACHE // 2, CACHE, 0).astype(jnp.int32)
    out_weight = scatter_about(arg_keys[11], (ATT_HEADS * HD, DOUT), (ATT_HEADS * HD) ** -0.5, 0.0625, ((0, 32),))
    return {"ssm_inputs": ssm_inputs, "step_decay": step_decay, "state_inputs": state_inputs, "state_readout": state_readout, "skip_gain": skip_gain, "norm_gain": norm_gain, "new_keys": new_keys, "new_values": new_values, "cache_keys": cache_keys, "cache_values": cache_values, "cache_len": cache_len, "out_weight": out_weight}


def reference(ssm_inputs, step_decay, state_inputs, state_readout, skip_gain, norm_gain, new_keys, new_values, cache_keys, cache_values, cache_len, out_weight):
    per_group = MH // GROUPS
    order = jnp.arange(TOKENS_PER_SLICE)
    causal = order[:, None] >= order[None, :]

    def ssd_slice(carried, index):
        begin = (index * TOKENS_PER_SLICE).astype(jnp.int32)
        inputs = lax.dynamic_slice_in_dim(ssm_inputs, begin, TOKENS_PER_SLICE, 0).reshape(TOKENS_PER_SLICE, GROUPS, per_group, P_SIZE)
        decay = lax.dynamic_slice_in_dim(step_decay, begin, TOKENS_PER_SLICE, 1)
        b_part = lax.dynamic_slice_in_dim(state_inputs, begin, TOKENS_PER_SLICE, 1).astype(jnp.float32)
        c_part = lax.dynamic_slice_in_dim(state_readout, begin, TOKENS_PER_SLICE, 1).astype(jnp.float32)
        cum = jnp.cumsum(decay, axis=1).reshape(GROUPS, per_group, TOKENS_PER_SLICE)
        gram = jnp.einsum('gtn,gsn->gts', c_part, b_part)
        diff = cum[..., :, None] - cum[..., None, :]
        seg = jnp.where(causal, jnp.exp(-jnp.where(causal, diff, 0.0)), 0.0)
        weights = lax.optimization_barrier((gram[:, None] * seg).astype(jnp.bfloat16)).astype(jnp.float32)
        inputs32 = inputs.astype(jnp.float32)
        y_intra = jnp.einsum('ghts,sghp->tghp', weights, inputs32)
        y_state = jnp.exp(-cum).transpose(2, 0, 1)[..., None] * jnp.einsum('gtn,ghpn->tghp', c_part, carried, precision=lax.Precision.HIGHEST)
        y_all = y_intra + y_state + skip_gain.reshape(GROUPS, per_group)[None, :, :, None] * inputs32
        scale = lax.rsqrt(lax.optimization_barrier(jnp.mean(y_all * y_all, axis=-1, keepdims=True)) + 1e-05)
        normed = (y_all * scale * norm_gain.reshape(GROUPS, per_group, P_SIZE)).astype(jnp.bfloat16).reshape(TOKENS_PER_SLICE, MH * P_SIZE)
        tail = jnp.exp(cum[..., -1:] - cum)
        weighted = lax.optimization_barrier((tail.transpose(2, 0, 1)[..., None] * inputs32).astype(jnp.bfloat16)).astype(jnp.float32)
        slice_state = jnp.einsum('sghp,gsn->ghpn', weighted, b_part)
        carried = jnp.exp(-cum[..., -1])[..., None, None] * carried + slice_state
        return (carried, normed)
    initial_condition = jnp.zeros((GROUPS, per_group, P_SIZE, STATE), jnp.float32)
    _, normed_all = lax.scan(ssd_slice, initial_condition, jnp.arange(N_PIPE).astype(jnp.int32))
    span = CACHE + TOKENS_PER_SLICE
    keys_all = jnp.concatenate([cache_keys.reshape(KV, N_PIPE, CACHE, HD), new_keys.reshape(KV, N_PIPE, TOKENS_PER_SLICE, HD)], axis=2).reshape(KV, N_PIPE * span, HD)
    values_all = jnp.concatenate([cache_values.reshape(KV, N_PIPE, CACHE, HD), new_values.reshape(KV, N_PIPE, TOKENS_PER_SLICE, HD)], axis=2).reshape(KV, N_PIPE * span, HD)
    rows_all = jnp.arange(N_PIPE * span)
    within = rows_all % span
    owner = rows_all // span
    valid = (within >= CACHE) | (within < cache_len[owner])
    per_kv = ATT_HEADS // KV

    def attend(index):
        slice_index = index // KV
        head = index % KV
        block = normed_all[slice_index].reshape(TOKENS_PER_SLICE, ATT_HEADS, HD)
        queries = lax.dynamic_slice_in_dim(block, (head * per_kv).astype(jnp.int32), per_kv, 1).astype(jnp.float32)
        stochastic_seeds = keys_all[head].astype(jnp.float32)
        values = values_all[head].astype(jnp.float32)
        scores = jnp.einsum('tqd,kd->qtk', queries, stochastic_seeds) * HD ** (-0.5)
        allowed = valid[None, :] & ((owner[None, :] < slice_index) | (owner[None, :] == slice_index) & ((within[None, :] < CACHE) | (within[None, :] - CACHE <= order[:, None])))
        scores = jnp.where(allowed[None], scores, -jnp.inf)
        top = lax.optimization_barrier(jnp.max(scores, axis=-1, keepdims=True))
        expo = jnp.exp(scores - top)
        total = lax.optimization_barrier(jnp.sum(expo, axis=-1))
        probs = lax.optimization_barrier(expo.astype(jnp.bfloat16)).astype(jnp.float32)
        result = jnp.einsum('qtk,kd->qtd', probs, values) / total[..., None]
        return result.astype(jnp.bfloat16)
    pieces = lax.map(attend, jnp.arange(N_PIPE * KV).astype(jnp.int32))
    attended = pieces.reshape(N_PIPE, KV, per_kv, TOKENS_PER_SLICE, HD).transpose(0, 3, 1, 2, 4).reshape(STREAM_ITEMS, ATT_HEADS * HD)
    return jnp.dot(attended, out_weight, preferred_element_type=jnp.float32).astype(jnp.bfloat16)
```

```python
import functools
import math

import jax
import jax.numpy as jnp
from jax import lax
from jax.experimental import pallas as pl
from jax.experimental.pallas import tpu as pltpu
from jax.sharding import Mesh
from jax.sharding import PartitionSpec as P

CACHE = 128
MH = 128
P_SIZE = 64
HD = 128
TOKENS = 256
SPAN = CACHE + TOKENS
ROWS = 2 * SPAN + 16
CHIPS = 8
HIDDEN = -1e30
SCALE = HD ** (-0.5) * math.log2(math.e)

AXES = ("x", "yh", "c", "yl", "za", "z1", "z0")
SIZES = (4, 2, 2, 2, 4, 2, 2)
PIPE = ("x", "yh", "c")
TENSOR = ("yl", "za", "z1", "z0")
CHIP = ("x", "yh")
NEAR = ("z1", "z0")
OWNERS = ("z1", "yl", "za")

bf16 = jnp.bfloat16
f32 = jnp.float32


def dot(a, b, contract=((1,), (0,))):
    return lax.dot_general(a, b, (contract, ((), ())), preferred_element_type=f32)


def thirds(value):
    high = value.astype(bf16)
    rest = value - high.astype(f32)
    middle = rest.astype(bf16)
    low = (rest - middle.astype(f32)).astype(bf16)
    return (low, middle, high)


def tri(transposed):
    first = lax.broadcasted_iota(jnp.int32, (TOKENS, TOKENS), 0)
    second = lax.broadcasted_iota(jnp.int32, (TOKENS, TOKENS), 1)
    return (first <= second) if transposed else (first >= second)


def cum_columns(decay):
    lower = tri(False).astype(f32).astype(bf16)
    return sum(dot(lower, part, ((1,), (1,))) for part in thirds(decay))


def cum_rows(decay):
    upper = tri(True).astype(f32).astype(bf16)
    return sum(dot(part, upper) for part in thirds(decay))


def low_lanes(rows):
    return lax.broadcasted_iota(jnp.int32, (rows, 2 * P_SIZE), 1) < P_SIZE


def spread(columns, half, rows):
    left, right = columns[:, 2 * half : 2 * half + 1], columns[:, 2 * half + 1 : 2 * half + 2]
    return jnp.where(low_lanes(rows), left, right)


def state_kernel(group_ref, x_ref, decay_ref, b_ref, out_ref):
    cum = cum_columns(decay_ref[...])
    last = cum[TOKENS - 1 :, :]
    tail = jnp.exp(last - cum)
    total = jnp.exp(-last)
    for half in range(2):
        inputs = x_ref[:, half * HD : (half + 1) * HD].astype(f32)
        weighted = (spread(tail, half, TOKENS) * inputs).astype(bf16)
        out_ref[half, 0:HD, :] = dot(b_ref[0], weighted, ((0,), (0,)))
        out_ref[half, HD : HD + 8, :] = spread(jnp.broadcast_to(total, (8, 4)), half, 8)


def pair_kernel(place_ref, both_ref, out_ref):
    first, second = both_ref[0, 0], both_ref[1, 0]
    decay = second[HD : HD + 1]
    state = first[0:HD] * decay + second[0:HD]
    total = first[HD:] * second[HD:]
    for copy in range(CHIPS):
        out_ref[copy, 0:HD, :] = state
        out_ref[copy, HD : HD + 8, :] = total


def scan_kernel(place_ref, all_ref, out_ref):
    chip = place_ref[0]
    state = jnp.zeros((HD, HD), f32)
    for k in range(CHIPS - 1):
        new = all_ref[k, HD : HD + 1] * state + all_ref[k, 0:HD]
        state = jnp.where(k < chip, new, state)
    out_ref[...] = state


def inside_kernel(group_ref, x_ref, decay_ref, b_ref, c_ref, gain_ref, y_ref, fade_ref):
    decay = decay_ref[...]
    columns, rows = cum_columns(decay), cum_rows(decay)
    causal = tri(False)
    gram = dot(c_ref[0], b_ref[0], ((1,), (1,)))
    fade = jnp.exp(-columns)
    for half in range(2):
        inputs = x_ref[:, half * HD : (half + 1) * HD]
        pieces = []
        for head in (2 * half, 2 * half + 1):
            diff = jnp.where(causal, columns[:, head : head + 1] - rows[head : head + 1, :], 0.0)
            weights = jnp.where(causal, gram * jnp.exp(-diff), 0.0).astype(bf16)
            pieces.append(dot(weights, inputs))
        low = low_lanes(TOKENS)
        skip = jnp.where(low_lanes(1), gain_ref[2 * half], gain_ref[2 * half + 1])
        y_ref[half] = jnp.where(low, pieces[0], pieces[1]) + skip * inputs.astype(f32)
        fade_ref[half] = spread(fade, half, TOKENS)


def query_kernel(place_ref, y_ref, fade_ref, c_ref, carried_ref, both_ref, gain_ref, *out_refs):
    core, near = place_ref[1], place_ref[2]
    readout = c_ref[0]
    low = low_lanes(TOKENS)
    halves = []
    for half in range(2):
        carried = carried_ref[half]
        after = both_ref[0, half, HD : HD + 1] * carried + both_ref[0, half, 0:HD]
        carried = jnp.where(core == 1, after, carried)
        from_state = sum(dot(readout, part) for part in thirds(carried))
        y = y_ref[half] + fade_ref[half] * from_state
        square = y * y
        left = jnp.sum(jnp.where(low, square, 0.0), axis=1, keepdims=True)
        right = jnp.sum(jnp.where(low, 0.0, square), axis=1, keepdims=True)
        mean = jnp.where(low, left, right) * (1.0 / P_SIZE)
        halves.append(y * lax.rsqrt(mean + 1e-05) * gain_ref[0:1, half * HD : (half + 1) * HD])
    sets = []
    for member in range(4):
        pieces = [
            jnp.concatenate([half[32 * i + 8 * member : 32 * i + 8 * member + 8] for i in range(8)], axis=0)
            for half in halves
        ]
        sets.append([piece.astype(bf16) for piece in pieces])
    for mine in range(4):

        @pl.when(near == mine)
        def _():
            for i in range(4):
                for half in range(2):
                    out_refs[i][:, half * HD : (half + 1) * HD] = sets[mine ^ i][half]


def pack_kernel(place_ref, ck_ref, nk_ref, cv_ref, nv_ref, len_ref, out_ref):
    slots = lax.broadcasted_iota(jnp.int32, (16, HD), 1)
    bias = jnp.where(slots < len_ref[0], 0.0, HIDDEN).astype(bf16)
    out_ref[0, 0:CACHE, :] = ck_ref[0]
    out_ref[0, CACHE:SPAN, :] = nk_ref[0]
    out_ref[0, SPAN : SPAN + CACHE, :] = cv_ref[0]
    out_ref[0, SPAN + CACHE : 2 * SPAN, :] = nv_ref[0]
    out_ref[0, 2 * SPAN :, :] = bias


def attend_kernel(place_ref, q0, q1, q2, q3, a_ref, b_ref, out_ref, scores_ref, q_ref, top_ref, sum_ref, acc_ref):
    chip, core, near = place_ref[0], place_ref[1], place_ref[2]
    count = q_ref.shape[0]
    for i, ref in enumerate((q0, q1, q2, q3)):
        for half in range(2):
            row = (2 * i + half) * 64
            q_ref[row : row + 64, :] = ref[:, half * HD : (half + 1) * HD]
    top_ref[...] = jnp.full((count, HD), -jnp.inf, f32)

    def score(kv_ref, k, side, extra, causal):
        keys = kv_ref[pl.ds(k, 1)][0]
        bias = keys[2 * SPAN : 2 * SPAN + 1, :].astype(f32) + extra
        raw = dot(q_ref[...], keys[0:SPAN], ((1,), (1,)))
        top = top_ref[...]
        for tile in range(SPAN // HD):
            part = raw[:, tile * HD : (tile + 1) * HD]
            if tile == 0:
                part = part + bias
            elif causal:
                row = lax.broadcasted_iota(jnp.int32, (count, HD), 0) % 64
                token = 32 * (row // 8) + 8 * near + row % 8
                key = lax.broadcasted_iota(jnp.int32, (count, HD), 1) + (tile - 1) * HD
                part = jnp.where(key <= token, part, HIDDEN)
            elif extra is not None:
                part = part + extra
            top = jnp.maximum(top, part)
            scores_ref[k, :, side * SPAN + tile * HD : side * SPAN + (tile + 1) * HD] = part
        top_ref[...] = top

    def early(k, carry):
        score(a_ref, k, 0, 0.0, False)
        score(b_ref, k, 1, 0.0, False)
        return carry

    lax.fori_loop(0, chip, early, 0)
    score(a_ref, chip, 0, 0.0, True)
    score(b_ref, chip, 1, jnp.where(core == 1, 0.0, HIDDEN), False)

    top = jnp.max(top_ref[...], axis=1, keepdims=True) * SCALE
    top_ref[...] = jnp.broadcast_to(top, (count, HD))
    sum_ref[...] = jnp.zeros((count, HD), f32)
    acc_ref[...] = jnp.zeros((count, HD), f32)

    def late(k, carry):
        top = top_ref[...]
        total = sum_ref[...]
        acc = acc_ref[...]
        for side, kv_ref in enumerate((a_ref, b_ref)):
            values = kv_ref[pl.ds(k, 1)][0][SPAN : 2 * SPAN]
            probs = []
            for tile in range(SPAN // HD):
                part = scores_ref[k, :, side * SPAN + tile * HD : side * SPAN + (tile + 1) * HD]
                expo = jnp.exp2(part * SCALE - top)
                total = total + expo
                probs.append(expo.astype(bf16))
            acc = acc + dot(jnp.concatenate(probs, axis=1), values)
        sum_ref[...] = total
        acc_ref[...] = acc
        return carry

    lax.fori_loop(0, chip + 1, late, 0)
    total = jnp.sum(sum_ref[...], axis=1, keepdims=True)
    result = (acc_ref[...] / total).astype(bf16)
    for i in range(4):
        for half in range(2):
            row = (2 * i + half) * 64
            out_ref[near ^ i, :, half * HD : (half + 1) * HD] = result[row : row + 64]


def project_kernel(place_ref, att_ref, own_ref, r1, r2, r3, s1, s2, s3, out_ref):
    near, core = place_ref[2], place_ref[1]

    def run(others):
        total = None
        for i, ref in enumerate((own_ref,) + others):
            heads = jnp.concatenate([att_ref[0, near ^ i], att_ref[1, near ^ i]], axis=0)
            term = dot(heads, ref[...])
            total = term if total is None else total + term
        out_ref[...] = total.astype(bf16)

    @pl.when(pl.program_id(0) == core)
    def _():
        run((r1, r2, r3))

    @pl.when(pl.program_id(0) != core)
    def _():
        run((s1, s2, s3))


def finish_kernel(parts_ref, out_ref):
    for half in range(2):
        total = parts_ref[8 * half].astype(f32)
        for i in range(1, 8):
            total = total + parts_ref[8 * half + i].astype(f32)
        width = parts_ref.shape[2]
        out_ref[:, half * width : (half + 1) * width] = total.astype(bf16)


def whole(shape):
    return pl.BlockSpec(shape, lambda *_: (0,) * len(shape))


SMEM = pl.BlockSpec(memory_space=pltpu.SMEM)


def call(kernel, scalars, args, in_specs, out_shape, out_specs, grid=(1,), scratch=(), flops=0, nbytes=1 << 12):
    return pl.pallas_call(
        kernel,
        out_shape=out_shape,
        grid_spec=pltpu.PrefetchScalarGridSpec(
            num_scalar_prefetch=1, grid=grid, in_specs=in_specs, out_specs=out_specs, scratch_shapes=scratch
        ),
        compiler_params=pltpu.CompilerParams(vmem_limit_bytes=40 * 1024 * 1024),
        cost_estimate=pl.CostEstimate(flops=flops, bytes_accessed=nbytes, transcendentals=0),
    )(scalars, *args)


def shape(*dims, dtype=f32):
    return jax.ShapeDtypeStruct(dims, dtype)


def swap(array, axis):
    return lax.ppermute(array, axis, [(0, 1), (1, 0)])


def flip(array, i):
    return lax.ppermute(array, NEAR, [(j, j ^ i) for j in range(4)])


def per_device(
    ssm_inputs,
    step_decay,
    state_inputs,
    state_readout,
    skip_gain,
    norm_gain,
    new_keys,
    new_values,
    cache_keys,
    cache_values,
    cache_len,
    out_weight,
):
    width = out_weight.shape[1] // 4
    core = lax.axis_index("c")
    near = lax.axis_index(NEAR)
    group = lax.axis_index(("yl", "za")).astype(jnp.int32)
    place = jnp.stack([lax.axis_index(CHIP), core, near, group]).astype(jnp.int32)
    of_group = lambda rows: pl.BlockSpec((1, rows, HD), lambda i, s: (s[3], 0, 0))

    own = call(
        state_kernel,
        place,
        (ssm_inputs, step_decay, state_inputs),
        [whole((TOKENS, 2 * HD)), whole((4, TOKENS)), of_group(TOKENS)],
        shape(2, HD + 8, HD),
        whole((2, HD + 8, HD)),
    )
    both = lax.all_gather(own, "c")
    pair = call(
        pair_kernel,
        place,
        (both,),
        [pl.BlockSpec((2, 1, HD + 8, HD), lambda i, s: (0, s[1], 0, 0))],
        shape(CHIPS, HD + 8, HD),
        whole((CHIPS, HD + 8, HD)),
    )
    out_weight, pair = lax.optimization_barrier((out_weight, pair))
    columns = lambda quarter: lax.dynamic_slice_in_dim(out_weight, quarter * width, width, 1)
    first = flip(columns(2 * (near // 2) + core), 1)
    second = columns(2 * (1 - near // 2) + core)
    pairs = lax.all_to_all(pair, CHIP, 0, 0, tiled=True)
    pairs, first, second = lax.optimization_barrier((pairs, first, second))
    second = flip(second, 2)
    entering = call(
        scan_kernel, place, (pairs,), [whole((CHIPS, HD + 8, HD))], shape(HD, HD), whole((HD, HD))
    )
    carried = lax.all_gather(entering, "c")

    inside, fade = call(
        inside_kernel,
        place,
        (ssm_inputs, step_decay, state_inputs, state_readout, skip_gain),
        [whole((TOKENS, 2 * HD)), whole((4, TOKENS)), of_group(TOKENS), of_group(TOKENS), SMEM],
        (shape(2, TOKENS, HD), shape(2, TOKENS, HD)),
        (whole((2, TOKENS, HD)), whole((2, TOKENS, HD))),
    )
    packed = call(
        pack_kernel,
        place,
        (cache_keys, new_keys, cache_values, new_values, cache_len),
        [of_group(CACHE), of_group(TOKENS), of_group(CACHE), of_group(TOKENS), SMEM],
        shape(CHIPS, ROWS, HD, dtype=bf16),
        pl.BlockSpec((1, ROWS, HD), lambda i, s: (i, 0, 0)),
        grid=(CHIPS,),
    )

    queries = call(
        query_kernel,
        place,
        (inside, fade, state_readout, carried, both, norm_gain.reshape(1, 2 * HD)),
        [
            whole((2, TOKENS, HD)),
            whole((2, TOKENS, HD)),
            of_group(TOKENS),
            whole((2, HD, HD)),
            whole((2, 2, HD + 8, HD)),
            whole((1, 2 * HD)),
        ],
        tuple(shape(64, 2 * HD, dtype=bf16) for _ in range(4)),
        tuple(whole((64, 2 * HD)) for _ in range(4)),
    )
    packed, _ = lax.optimization_barrier((packed, entering))
    same = lax.all_to_all(packed, CHIP, 0, 0, tiled=True)
    queries = [queries[0]] + [flip(queries[i], i) for i in (1, 2, 3)]
    same, queries, second = lax.optimization_barrier((same, queries, second))
    other = swap(same, "c")
    third = flip(second, 1)
    swapped = [swap(part, "c") for part in (first, second)]

    attended = call(
        attend_kernel,
        place,
        (*queries, same, other),
        [whole((64, 2 * HD))] * 4 + [whole((CHIPS, ROWS, HD))] * 2,
        shape(4, 64, 2 * HD, dtype=bf16),
        whole((4, 64, 2 * HD)),
        scratch=[
            pltpu.VMEM((CHIPS, 512, 2 * SPAN), f32),
            pltpu.VMEM((512, HD), bf16),
            pltpu.VMEM((512, HD), f32),
            pltpu.VMEM((512, HD), f32),
            pltpu.VMEM((512, HD), f32),
        ],
    )
    attended, third = lax.optimization_barrier((attended, third))
    attended = lax.all_gather(attended, "z1")
    received = (first, second, third)
    swapped.append(swap(third, "c"))
    piece = whole((2 * HD, width))
    partial = call(
        project_kernel,
        place,
        (attended, out_weight, *received, *swapped),
        [whole((2, 4, 64, 2 * HD)), pl.BlockSpec((2 * HD, width), lambda i, s: (0, 2 * (s[2] // 2) + i))] + [piece] * 6,
        shape(128, 2 * width, dtype=bf16),
        pl.BlockSpec((128, width), lambda i, s: (0, i)),
        grid=(2,),
    )
    parts = lax.all_to_all(partial.reshape(16, 8, 2 * width), OWNERS, 0, 0, tiled=True)
    return pl.pallas_call(
        finish_kernel,
        out_shape=shape(8, 4 * width, dtype=bf16),
        compiler_params=pltpu.CompilerParams(vmem_limit_bytes=40 * 1024 * 1024),
    )(parts)


def solution(mesh):
    fine = Mesh(mesh.devices.reshape(SIZES), AXES)
    placed = (
        P(PIPE, TENSOR),
        P(TENSOR, PIPE),
        P(None, PIPE, None),
        P(None, PIPE, None),
        P(TENSOR),
        P(TENSOR),
        P(None, PIPE, None),
        P(None, PIPE, None),
        P(None, PIPE, None),
        P(None, PIPE, None),
        P(PIPE),
        P(TENSOR, None),
    )
    return jax.shard_map(
        per_device,
        mesh=fine,
        in_specs=placed,
        out_specs=P(PIPE + TENSOR, None),
        check_vma=False,
    )
```

```python
import functools
import math

import jax
import jax.numpy as jnp
from jax import lax
from jax.experimental import pallas as pl
from jax.experimental.pallas import tpu as pltpu
from jax.sharding import Mesh
from jax.sharding import PartitionSpec as P

CACHE = 128
MH = 128
P_SIZE = 64
HD = 128
TOKENS = 256
SPAN = CACHE + TOKENS
HEAD = 2 * HD + 16
ROWS = HEAD + 2 * SPAN
CHIPS = 8
HIDDEN = -1e30
SCALE = HD ** (-0.5) * math.log2(math.e)

AXES = ("x", "yh", "c", "yl", "za", "z1", "z0")
SIZES = (4, 2, 2, 2, 4, 2, 2)
PIPE = ("x", "yh", "c")
TENSOR = ("yl", "za", "z1", "z0")
CHIP = ("x", "yh")
NEAR = ("z1", "z0")
OWNERS = ("za", "z1")

bf16 = jnp.bfloat16
f32 = jnp.float32


def dot(a, b, contract=((1,), (0,))):
    return lax.dot_general(a, b, (contract, ((), ())), preferred_element_type=f32)


def thirds(value):
    high = value.astype(bf16)
    rest = value - high.astype(f32)
    middle = rest.astype(bf16)
    low = (rest - middle.astype(f32)).astype(bf16)
    return (low, middle, high)


def tri(transposed):
    first = lax.broadcasted_iota(jnp.int32, (TOKENS, TOKENS), 0)
    second = lax.broadcasted_iota(jnp.int32, (TOKENS, TOKENS), 1)
    return (first <= second) if transposed else (first >= second)


def cum_columns(decay):
    lower = tri(False).astype(f32).astype(bf16)
    return sum(dot(lower, part, ((1,), (1,))) for part in thirds(decay))


def cum_rows(decay):
    upper = tri(True).astype(f32).astype(bf16)
    return sum(dot(part, upper) for part in thirds(decay))


def low_lanes(rows):
    return lax.broadcasted_iota(jnp.int32, (rows, 2 * P_SIZE), 1) < P_SIZE


def spread(columns, half, rows):
    left, right = columns[:, 2 * half : 2 * half + 1], columns[:, 2 * half + 1 : 2 * half + 2]
    return jnp.where(low_lanes(rows), left, right)


def state_kernel(group_ref, x_ref, decay_ref, b_ref, out_ref):
    cum = cum_columns(decay_ref[...])
    last = cum[TOKENS - 1 :, :]
    tail = jnp.exp(last - cum)
    total = jnp.exp(-last)
    for half in range(2):
        inputs = x_ref[:, half * HD : (half + 1) * HD].astype(f32)
        weighted = (spread(tail, half, TOKENS) * inputs).astype(bf16)
        out_ref[half, 0:HD, :] = dot(b_ref[0], weighted, ((0,), (0,)))
        out_ref[half, HD : HD + 8, :] = spread(jnp.broadcast_to(total, (8, 4)), half, 8)


def spread_copies(held, out_ref, begin, sems):
    rows = held.shape[0]
    copies = [pltpu.make_async_copy(held, out_ref.at[k, begin : begin + rows], sems.at[k]) for k in range(CHIPS)]
    for copy in copies:
        copy.start()
    for copy in copies:
        copy.wait()


def fill_kernel(place_ref, ck_ref, nk_ref, cv_ref, nv_ref, out_ref, held, sems):
    for begin, ref in ((0, ck_ref), (CACHE, nk_ref), (SPAN, cv_ref), (SPAN + CACHE, nv_ref)):
        held[begin : begin + ref.shape[1], :] = ref[0]
    spread_copies(held, out_ref, HEAD, sems)


def pack_kernel(place_ref, both_ref, len_ref, filled_ref, out_ref, held, sems):
    first, second = both_ref[0, 0], both_ref[1, 0]
    state = first[0:HD] * second[HD : HD + 1] + second[0:HD]
    high = state.astype(bf16)
    held[0:HD, :] = high
    held[HD : 2 * HD, :] = (state - high.astype(f32)).astype(bf16)
    slots = lax.broadcasted_iota(jnp.int32, (16, HD), 1)
    row = lax.broadcasted_iota(jnp.int32, (16, HD), 0)
    tile = jnp.where(slots < len_ref[0], 0.0, HIDDEN)
    for i, part in enumerate(thirds(first[HD : HD + 1] * second[HD : HD + 1])):
        tile = jnp.where(row == i + 1, part.astype(f32), tile)
    held[2 * HD : HEAD, :] = tile.astype(bf16)
    spread_copies(held, out_ref, 0, sems)


def scan_kernel(place_ref, all_ref, out_ref):
    chip = place_ref[0]
    state = jnp.zeros((HD, HD), f32)
    for k in range(CHIPS - 1):
        tile = all_ref[k, 2 * HD : HEAD, :].astype(f32)
        decay = tile[1:2] + tile[2:3] + tile[3:4]
        here = all_ref[k, 0:HD, :].astype(f32) + all_ref[k, HD : 2 * HD, :].astype(f32)
        state = jnp.where(k < chip, decay * state + here, state)
    out_ref[...] = state


def inside_kernel(group_ref, x_ref, decay_ref, b_ref, c_ref, gain_ref, y_ref, fade_ref):
    decay = decay_ref[...]
    columns, rows = cum_columns(decay), cum_rows(decay)
    causal = tri(False)
    gram = dot(c_ref[0], b_ref[0], ((1,), (1,)))
    fade = jnp.exp(-columns)
    for half in range(2):
        inputs = x_ref[:, half * HD : (half + 1) * HD]
        pieces = []
        for head in (2 * half, 2 * half + 1):
            diff = jnp.where(causal, columns[:, head : head + 1] - rows[head : head + 1, :], 0.0)
            weights = jnp.where(causal, gram * jnp.exp(-diff), 0.0).astype(bf16)
            pieces.append(dot(weights, inputs))
        low = low_lanes(TOKENS)
        skip = jnp.where(low_lanes(1), gain_ref[2 * half], gain_ref[2 * half + 1])
        y_ref[half] = jnp.where(low, pieces[0], pieces[1]) + skip * inputs.astype(f32)
        fade_ref[half] = spread(fade, half, TOKENS)


def query_kernel(place_ref, y_ref, fade_ref, c_ref, carried_ref, both_ref, gain_ref, out_ref):
    core = place_ref[1]
    readout = c_ref[0]
    low = low_lanes(TOKENS)
    for half in range(2):
        carried = carried_ref[half]
        after = both_ref[0, half, HD : HD + 1] * carried + both_ref[0, half, 0:HD]
        carried = jnp.where(core == 1, after, carried)
        from_state = sum(dot(readout, part) for part in thirds(carried))
        y = y_ref[half] + fade_ref[half] * from_state
        square = y * y
        left = jnp.sum(jnp.where(low, square, 0.0), axis=1, keepdims=True)
        right = jnp.sum(jnp.where(low, 0.0, square), axis=1, keepdims=True)
        mean = jnp.where(low, left, right) * (1.0 / P_SIZE)
        normed = y * lax.rsqrt(mean + 1e-05) * gain_ref[0:1, half * HD : (half + 1) * HD]
        out_ref[half * TOKENS : (half + 1) * TOKENS, :] = normed.astype(bf16)


def attend_kernel(place_ref, q_ref, a_ref, b_ref, out_ref, scores_ref, top_ref, sum_ref, acc_ref):
    chip, core = place_ref[0], place_ref[1]
    count = q_ref.shape[0]
    sides = (a_ref, b_ref)
    top_ref[...] = jnp.full((count, HD), -jnp.inf, f32)

    def score(k, side, extra, causal):
        bias = sides[side][k, 2 * HD : HEAD, :].astype(f32)[0:1]
        raw = dot(q_ref[...], sides[side][k, HEAD : HEAD + SPAN, :], ((1,), (1,)))
        top = top_ref[...]
        for tile in range(SPAN // HD):
            part = raw[:, tile * HD : (tile + 1) * HD]
            if tile == 0:
                part = part + (bias if extra is None else bias + extra)
            elif causal:
                token = lax.broadcasted_iota(jnp.int32, (count, HD), 0) % TOKENS
                key = lax.broadcasted_iota(jnp.int32, (count, HD), 1) + (tile - 1) * HD
                part = jnp.where(key <= token, part, HIDDEN)
            elif extra is not None:
                part = part + extra
            top = jnp.maximum(top, part)
            scores_ref[k, :, side * SPAN + tile * HD : side * SPAN + (tile + 1) * HD] = part
        top_ref[...] = top

    def early(k, carry):
        score(k, 0, None, False)
        score(k, 1, None, False)
        return carry

    lax.fori_loop(0, chip, early, 0)
    score(chip, 0, None, True)
    score(chip, 1, jnp.where(core == 1, 0.0, HIDDEN), False)

    top = jnp.max(top_ref[...], axis=1, keepdims=True) * SCALE
    top_ref[...] = jnp.broadcast_to(top, (count, HD))
    sum_ref[...] = jnp.zeros((count, HD), f32)
    acc_ref[...] = jnp.zeros((count, HD), f32)

    def late(k, carry):
        top = top_ref[...]
        total = sum_ref[...]
        acc = acc_ref[...]
        for side in range(2):
            probs = []
            for tile in range(SPAN // HD):
                part = scores_ref[k, :, side * SPAN + tile * HD : side * SPAN + (tile + 1) * HD]
                expo = jnp.exp2(part * SCALE - top)
                total = total + expo
                probs.append(expo.astype(bf16))
            acc = acc + dot(jnp.concatenate(probs, axis=1), sides[side][k, HEAD + SPAN :, :])
        sum_ref[...] = total
        acc_ref[...] = acc
        return carry

    lax.fori_loop(0, chip + 1, late, 0)
    total = jnp.sum(sum_ref[...], axis=1, keepdims=True)
    result = acc_ref[...] / total
    for z0 in range(2):
        for half in range(2):
            blocks = [16 * yl + 4 * za + 2 * z1 + z0 for yl in range(2) for za in range(4) for z1 in range(2)]
            rows = [half * TOKENS + 8 * block for block in blocks]
            piece = jnp.concatenate([result[row : row + 8] for row in rows], axis=0).astype(bf16)
            for z1 in range(2):
                out_ref[2 * z1 + z0, :, half * HD : (half + 1) * HD] = piece


def project_kernel(place_ref, att_ref, own_ref, r1, r2, r3, s1, s2, s3, keep_ref, send_ref):
    near, core, side = place_ref[2], place_ref[1], place_ref[3] // 4
    rows, width = keep_ref.shape[0], r1.shape[1]

    def run(others, begin):
        total = dot(att_ref[near], own_ref[:, begin : begin + width])
        for i, ref in enumerate(others):
            total = total + dot(att_ref[near ^ (i + 1)], ref[...])
        total = total.astype(bf16)

        @pl.when(side == 0)
        def _():
            keep_ref[:, begin : begin + width] = total[:rows]
            send_ref[:, begin : begin + width] = total[rows:]

        @pl.when(side == 1)
        def _():
            keep_ref[:, begin : begin + width] = total[rows:]
            send_ref[:, begin : begin + width] = total[:rows]

    @pl.when(core == 0)
    def _():
        run((r1, r2, r3), 0)
        run((s1, s2, s3), width)

    @pl.when(core == 1)
    def _():
        run((s1, s2, s3), 0)
        run((r1, r2, r3), width)


def add_kernel(first_ref, second_ref, out_ref):
    out_ref[...] = (first_ref[...].astype(f32) + second_ref[...].astype(f32)).astype(bf16)


def finish_kernel(parts_ref, out_ref):
    for half in range(2):
        total = parts_ref[half].astype(f32)
        for i in range(1, 4):
            total = total + parts_ref[2 * i + half].astype(f32)
        width = parts_ref.shape[2]
        out_ref[:, half * width : (half + 1) * width] = total.astype(bf16)


def whole(shape):
    return pl.BlockSpec(shape, lambda *_: (0,) * len(shape))


SMEM = pl.BlockSpec(memory_space=pltpu.SMEM)


def call(kernel, scalars, args, in_specs, out_shape, out_specs, grid=(1,), scratch=(), room=40, aliases=None):
    return pl.pallas_call(
        kernel,
        out_shape=out_shape,
        grid_spec=pltpu.PrefetchScalarGridSpec(
            num_scalar_prefetch=1, grid=grid, in_specs=in_specs, out_specs=out_specs, scratch_shapes=scratch
        ),
        input_output_aliases=aliases or {},
        compiler_params=pltpu.CompilerParams(vmem_limit_bytes=room * 1024 * 1024),
        cost_estimate=pl.CostEstimate(flops=0, bytes_accessed=1 << 12, transcendentals=0),
    )(scalars, *args)


def shape(*dims, dtype=f32):
    return jax.ShapeDtypeStruct(dims, dtype)


def swap(array, axis):
    return lax.ppermute(array, axis, [(0, 1), (1, 0)])


def flip(array, i):
    return lax.ppermute(array, NEAR, [(j, j ^ i) for j in range(4)])


def per_device(
    ssm_inputs,
    step_decay,
    state_inputs,
    state_readout,
    skip_gain,
    norm_gain,
    new_keys,
    new_values,
    cache_keys,
    cache_values,
    cache_len,
    out_weight,
):
    width = out_weight.shape[1] // 4
    core = lax.axis_index("c")
    near = lax.axis_index(NEAR)
    group = lax.axis_index(("yl", "za")).astype(jnp.int32)
    place = jnp.stack([lax.axis_index(CHIP), core, near, group]).astype(jnp.int32)
    of_group = lambda rows: pl.BlockSpec((1, rows, HD), lambda i, s: (s[3], 0, 0))

    filled = call(
        fill_kernel,
        place,
        (cache_keys, new_keys, cache_values, new_values),
        [of_group(CACHE), of_group(TOKENS), of_group(CACHE), of_group(TOKENS)],
        shape(CHIPS, ROWS, HD, dtype=bf16),
        pl.BlockSpec(memory_space=pl.ANY),
        scratch=[pltpu.VMEM((2 * SPAN, HD), bf16), pltpu.SemaphoreType.DMA((CHIPS,))],
        room=60,
    )
    place, filled = lax.optimization_barrier((place, filled))

    own = call(
        state_kernel,
        place,
        (ssm_inputs, step_decay, state_inputs),
        [whole((TOKENS, 2 * HD)), whole((4, TOKENS)), of_group(TOKENS)],
        shape(2, HD + 8, HD),
        whole((2, HD + 8, HD)),
    )
    both = lax.all_gather(own, "c")
    packed = call(
        pack_kernel,
        place,
        (both, cache_len, filled),
        [
            pl.BlockSpec((2, 1, HD + 8, HD), lambda i, s: (0, s[1], 0, 0)),
            SMEM,
            pl.BlockSpec(memory_space=pl.ANY),
        ],
        shape(CHIPS, ROWS, HD, dtype=bf16),
        pl.BlockSpec(memory_space=pl.ANY),
        scratch=[pltpu.VMEM((HEAD, HD), bf16), pltpu.SemaphoreType.DMA((CHIPS,))],
        room=60,
        aliases={3: 0},
    )

    columns = lambda quarter: lax.dynamic_slice_in_dim(out_weight, quarter * width, width, 1)
    second = flip(columns(2 * (1 - near // 2) + core), 2)
    first = flip(columns(2 * (near // 2) + core), 1)
    third = flip(second, 1)
    own_columns = lax.dynamic_slice_in_dim(out_weight, 2 * (near // 2) * width, 2 * width, 1)
    same = lax.all_to_all(packed, CHIP, 0, 0, tiled=True)
    inside, fade = call(
        inside_kernel,
        place,
        (ssm_inputs, step_decay, state_inputs, state_readout, skip_gain),
        [whole((TOKENS, 2 * HD)), whole((4, TOKENS)), of_group(TOKENS), of_group(TOKENS), SMEM],
        (shape(2, TOKENS, HD), shape(2, TOKENS, HD)),
        (whole((2, TOKENS, HD)), whole((2, TOKENS, HD))),
    )
    same, first, second, inside, fade, own_columns = lax.optimization_barrier(
        (same, first, second, inside, fade, own_columns)
    )
    other = swap(same, "c")
    entering = call(
        scan_kernel,
        place,
        (same,),
        [pl.BlockSpec((CHIPS, HEAD, HD), lambda i, s: (0, 0, 0))],
        shape(HD, HD),
        whole((HD, HD)),
    )
    carried = lax.all_gather(entering, "c")
    queries = call(
        query_kernel,
        place,
        (inside, fade, state_readout, carried, both, norm_gain.reshape(1, 2 * HD)),
        [
            whole((2, TOKENS, HD)),
            whole((2, TOKENS, HD)),
            of_group(TOKENS),
            whole((2, HD, HD)),
            whole((2, 2, HD + 8, HD)),
            whole((1, 2 * HD)),
        ],
        shape(2 * TOKENS, HD, dtype=bf16),
        whole((2 * TOKENS, HD)),
    )

    attended = call(
        attend_kernel,
        place,
        (queries, same, other),
        [whole((2 * TOKENS, HD))] + [whole((CHIPS, ROWS, HD))] * 2,
        shape(4, TOKENS // 2, 2 * HD, dtype=bf16),
        whole((4, TOKENS // 2, 2 * HD)),
        scratch=[
            pltpu.VMEM((CHIPS, 2 * TOKENS, 2 * SPAN), f32),
            pltpu.VMEM((2 * TOKENS, HD), f32),
            pltpu.VMEM((2 * TOKENS, HD), f32),
            pltpu.VMEM((2 * TOKENS, HD), f32),
        ],
    )
    attended, first, second = lax.optimization_barrier((attended, first, second))
    received = (first, second, third)
    swapped = [swap(part, "c") for part in received]
    attended = lax.all_to_all(attended, NEAR, 0, 0, tiled=True)
    vmem = pl.BlockSpec(memory_space=pltpu.VMEM)
    keep, send = call(
        project_kernel,
        place,
        (attended, own_columns, *received, *swapped),
        [vmem] * 8,
        (shape(64, 2 * width, dtype=bf16),) * 2,
        (vmem,) * 2,
    )
    simple = functools.partial(pl.pallas_call, compiler_params=pltpu.CompilerParams(vmem_limit_bytes=40 * 1024 * 1024))
    partial = simple(add_kernel, out_shape=shape(64, 2 * width, dtype=bf16))(keep, swap(send, "yl"))
    parts = lax.all_to_all(partial.reshape(8, 8, 2 * width), OWNERS, 0, 0, tiled=True)
    return simple(finish_kernel, out_shape=shape(8, 4 * width, dtype=bf16))(parts)


def solution(mesh):
    fine = Mesh(mesh.devices.reshape(SIZES), AXES)
    placed = (
        P(PIPE, TENSOR),
        P(TENSOR, PIPE),
        P(None, PIPE, None),
        P(None, PIPE, None),
        P(TENSOR),
        P(TENSOR),
        P(None, PIPE, None),
        P(None, PIPE, None),
        P(None, PIPE, None),
        P(None, PIPE, None),
        P(PIPE),
        P(TENSOR, None),
    )
    return jax.shard_map(
        per_device,
        mesh=fine,
        in_specs=placed,
        out_specs=P(PIPE + TENSOR, None),
        check_vma=False,
    )
```

```python
import functools
import math

import jax
import jax.numpy as jnp
from jax import lax
from jax.experimental import pallas as pl
from jax.experimental.pallas import tpu as pltpu
from jax.sharding import Mesh
from jax.sharding import PartitionSpec as P

CACHE = 128
MH = 128
P_SIZE = 64
HD = 128
TOKENS = 256
SPAN = CACHE + TOKENS
HEAD = 2 * HD + 16
ROWS = HEAD + 2 * SPAN
CHIPS = 8
HIDDEN = -1e30
SCALE = HD ** (-0.5) * math.log2(math.e)

AXES = ("x", "yh", "c", "yl", "za", "z1", "z0")
SIZES = (4, 2, 2, 2, 4, 2, 2)
PIPE = ("x", "yh", "c")
TENSOR = ("yl", "za", "z1", "z0")
CHIP = ("x", "yh")
NEAR = ("z1", "z0")
OWNERS = ("za", "z1")

bf16 = jnp.bfloat16
f32 = jnp.float32


def dot(a, b, contract=((1,), (0,))):
    return lax.dot_general(a, b, (contract, ((), ())), preferred_element_type=f32)


def thirds(value):
    high = value.astype(bf16)
    rest = value - high.astype(f32)
    middle = rest.astype(bf16)
    low = (rest - middle.astype(f32)).astype(bf16)
    return (low, middle, high)


def tri(transposed):
    first = lax.broadcasted_iota(jnp.int32, (TOKENS, TOKENS), 0)
    second = lax.broadcasted_iota(jnp.int32, (TOKENS, TOKENS), 1)
    return (first <= second) if transposed else (first >= second)


def cum_columns(decay):
    lower = tri(False).astype(f32).astype(bf16)
    return sum(dot(lower, part, ((1,), (1,))) for part in thirds(decay))


def cum_rows(decay):
    upper = tri(True).astype(f32).astype(bf16)
    return sum(dot(part, upper) for part in thirds(decay))


def low_lanes(rows):
    return lax.broadcasted_iota(jnp.int32, (rows, 2 * P_SIZE), 1) < P_SIZE


def spread(columns, half, rows):
    left, right = columns[:, 2 * half : 2 * half + 1], columns[:, 2 * half + 1 : 2 * half + 2]
    return jnp.where(low_lanes(rows), left, right)


def state_kernel(group_ref, x_ref, decay_ref, b_ref, out_ref):
    cum = cum_columns(decay_ref[...])
    last = cum[TOKENS - 1 :, :]
    tail = jnp.exp(last - cum)
    total = jnp.exp(-last)
    for half in range(2):
        inputs = x_ref[:, half * HD : (half + 1) * HD].astype(f32)
        weighted = (spread(tail, half, TOKENS) * inputs).astype(bf16)
        out_ref[half, 0:HD, :] = dot(b_ref[0], weighted, ((0,), (0,)))
        out_ref[half, HD : HD + 8, :] = spread(jnp.broadcast_to(total, (8, 4)), half, 8)


def spread_copies(held, out_ref, begin, sems):
    rows = held.shape[0]
    copies = [pltpu.make_async_copy(held, out_ref.at[k, begin : begin + rows], sems.at[k]) for k in range(CHIPS)]
    for copy in copies:
        copy.start()
    for copy in copies:
        copy.wait()


def spread_copies(held, out_ref, begin, sems):
    rows = held.shape[0]
    copies = [pltpu.make_async_copy(held, out_ref.at[k, begin : begin + rows], sems.at[k]) for k in range(CHIPS)]
    for copy in copies:
        copy.start()
    return copies


def fill_kernel(place_ref, ck_ref, nk_ref, cv_ref, nv_ref, w1_ref, w2_ref, out_ref, out1_ref, out2_ref, held, sems):
    for begin, ref in ((0, ck_ref), (CACHE, nk_ref), (SPAN, cv_ref), (SPAN + CACHE, nv_ref)):
        held[begin : begin + ref.shape[1], :] = ref[0]
    copies = spread_copies(held, out_ref, HEAD, sems)
    out1_ref[...] = w1_ref[...]
    out2_ref[...] = w2_ref[...]
    for copy in copies:
        copy.wait()


def pack_kernel(place_ref, both_ref, len_ref, filled_ref, out_ref, held, sems):
    first, second = both_ref[0, 0], both_ref[1, 0]
    state = first[0:HD] * second[HD : HD + 1] + second[0:HD]
    high = state.astype(bf16)
    held[0:HD, :] = high
    held[HD : 2 * HD, :] = (state - high.astype(f32)).astype(bf16)
    slots = lax.broadcasted_iota(jnp.int32, (16, HD), 1)
    row = lax.broadcasted_iota(jnp.int32, (16, HD), 0)
    tile = jnp.where(slots < len_ref[0], 0.0, HIDDEN)
    for i, part in enumerate(thirds(first[HD : HD + 1] * second[HD : HD + 1])):
        tile = jnp.where(row == i + 1, part.astype(f32), tile)
    held[2 * HD : HEAD, :] = tile.astype(bf16)
    for copy in spread_copies(held, out_ref, 0, sems):
        copy.wait()


def scan_kernel(place_ref, all_ref, out_ref):
    chip = place_ref[0]
    state = jnp.zeros((HD, HD), f32)
    for k in range(CHIPS - 1):
        tile = all_ref[k, 2 * HD : HEAD, :].astype(f32)
        decay = tile[1:2] + tile[2:3] + tile[3:4]
        here = all_ref[k, 0:HD, :].astype(f32) + all_ref[k, HD : 2 * HD, :].astype(f32)
        state = jnp.where(k < chip, decay * state + here, state)
    out_ref[...] = state


def inside_kernel(group_ref, x_ref, decay_ref, b_ref, c_ref, gain_ref, y_ref):
    decay = decay_ref[...]
    columns, rows = cum_columns(decay), cum_rows(decay)
    causal = tri(False)
    gram = dot(c_ref[0], b_ref[0], ((1,), (1,)))
    for half in range(2):
        inputs = x_ref[:, half * HD : (half + 1) * HD]
        pieces = []
        for head in (2 * half, 2 * half + 1):
            diff = jnp.where(causal, columns[:, head : head + 1] - rows[head : head + 1, :], 0.0)
            weights = jnp.where(causal, gram * jnp.exp(-diff), 0.0).astype(bf16)
            pieces.append(dot(weights, inputs))
        low = low_lanes(TOKENS)
        skip = jnp.where(low_lanes(1), gain_ref[2 * half], gain_ref[2 * half + 1])
        y_ref[half] = jnp.where(low, pieces[0], pieces[1]) + skip * inputs.astype(f32)


def query_kernel(place_ref, y_ref, decay_ref, c_ref, carried_ref, both_ref, gain_ref, out_ref):
    core = place_ref[1]
    readout = c_ref[0]
    low = low_lanes(TOKENS)
    fade = jnp.exp(-cum_columns(decay_ref[...]))
    for half in range(2):
        carried = carried_ref[half]
        after = both_ref[0, half, HD : HD + 1] * carried + both_ref[0, half, 0:HD]
        carried = jnp.where(core == 1, after, carried)
        from_state = sum(dot(readout, part) for part in thirds(carried))
        y = y_ref[half] + spread(fade, half, TOKENS) * from_state
        square = y * y
        left = jnp.sum(jnp.where(low, square, 0.0), axis=1, keepdims=True)
        right = jnp.sum(jnp.where(low, 0.0, square), axis=1, keepdims=True)
        mean = jnp.where(low, left, right) * (1.0 / P_SIZE)
        normed = y * lax.rsqrt(mean + 1e-05) * gain_ref[0:1, half * HD : (half + 1) * HD]
        out_ref[half * TOKENS : (half + 1) * TOKENS, :] = normed.astype(bf16)


def attend_kernel(place_ref, q_ref, a_ref, b_ref, out_ref, scores_ref, top_ref, sum_ref, acc_ref):
    chip, core = place_ref[0], place_ref[1]
    count = q_ref.shape[0]
    sides = (a_ref, b_ref)
    top_ref[...] = jnp.full((count, HD), -jnp.inf, f32)

    def score(k, side, extra, causal):
        bias = sides[side][k, 2 * HD : HEAD, :].astype(f32)[0:1]
        raw = dot(q_ref[...], sides[side][k, HEAD : HEAD + SPAN, :], ((1,), (1,)))
        top = top_ref[...]
        for tile in range(SPAN // HD):
            part = raw[:, tile * HD : (tile + 1) * HD]
            if tile == 0:
                part = part + (bias if extra is None else bias + extra)
            elif causal:
                token = lax.broadcasted_iota(jnp.int32, (count, HD), 0) % TOKENS
                key = lax.broadcasted_iota(jnp.int32, (count, HD), 1) + (tile - 1) * HD
                part = jnp.where(key <= token, part, HIDDEN)
            elif extra is not None:
                part = part + extra
            top = jnp.maximum(top, part)
            scores_ref[k, :, side * SPAN + tile * HD : side * SPAN + (tile + 1) * HD] = part
        top_ref[...] = top

    def early(k, carry):
        score(k, 0, None, False)
        score(k, 1, None, False)
        return carry

    lax.fori_loop(0, chip, early, 0)
    score(chip, 0, None, True)
    score(chip, 1, jnp.where(core == 1, 0.0, HIDDEN), False)

    top = jnp.max(top_ref[...], axis=1, keepdims=True) * SCALE
    top_ref[...] = jnp.broadcast_to(top, (count, HD))
    sum_ref[...] = jnp.zeros((count, HD), f32)
    acc_ref[...] = jnp.zeros((count, HD), f32)

    def late(k, carry):
        top = top_ref[...]
        total = sum_ref[...]
        acc = acc_ref[...]
        for side in range(2):
            probs = []
            for tile in range(SPAN // HD):
                part = scores_ref[k, :, side * SPAN + tile * HD : side * SPAN + (tile + 1) * HD]
                expo = jnp.exp2(part * SCALE - top)
                total = total + expo
                probs.append(expo.astype(bf16))
            acc = acc + dot(jnp.concatenate(probs, axis=1), sides[side][k, HEAD + SPAN :, :])
        sum_ref[...] = total
        acc_ref[...] = acc
        return carry

    lax.fori_loop(0, chip + 1, late, 0)
    total = jnp.sum(sum_ref[...], axis=1, keepdims=True)
    result = acc_ref[...] / total
    for z0 in range(2):
        for half in range(2):
            blocks = [16 * yl + 4 * za + 2 * z1 + z0 for yl in range(2) for za in range(4) for z1 in range(2)]
            rows = [half * TOKENS + 8 * block for block in blocks]
            piece = jnp.concatenate([result[row : row + 8] for row in rows], axis=0).astype(bf16)
            for z1 in range(2):
                out_ref[2 * z1 + z0, :, half * HD : (half + 1) * HD] = piece


def project_kernel(place_ref, att_ref, own_ref, r1, r2, r3, s1, s2, s3, keep_ref, send_ref):
    near, core, side = place_ref[2], place_ref[1], place_ref[3] // 4
    rows, width = keep_ref.shape[0], r1.shape[1]

    def run(others, begin):
        total = dot(att_ref[near], own_ref[:, begin : begin + width])
        for i, ref in enumerate(others):
            total = total + dot(att_ref[near ^ (i + 1)], ref[...])
        total = total.astype(bf16)

        @pl.when(side == 0)
        def _():
            keep_ref[:, begin : begin + width] = total[:rows]
            send_ref[:, begin : begin + width] = total[rows:]

        @pl.when(side == 1)
        def _():
            keep_ref[:, begin : begin + width] = total[rows:]
            send_ref[:, begin : begin + width] = total[:rows]

    @pl.when(core == 0)
    def _():
        run((r1, r2, r3), 0)
        run((s1, s2, s3), width)

    @pl.when(core == 1)
    def _():
        run((s1, s2, s3), 0)
        run((r1, r2, r3), width)


def add_kernel(first_ref, second_ref, out_ref):
    out_ref[...] = (first_ref[...].astype(f32) + second_ref[...].astype(f32)).astype(bf16)


def finish_kernel(parts_ref, out_ref):
    for half in range(2):
        total = parts_ref[half].astype(f32)
        for i in range(1, 4):
            total = total + parts_ref[2 * i + half].astype(f32)
        width = parts_ref.shape[2]
        out_ref[:, half * width : (half + 1) * width] = total.astype(bf16)


def whole(shape):
    return pl.BlockSpec(shape, lambda *_: (0,) * len(shape))


SMEM = pl.BlockSpec(memory_space=pltpu.SMEM)


def call(kernel, scalars, args, in_specs, out_shape, out_specs, grid=(1,), scratch=(), room=16, aliases=None):
    return pl.pallas_call(
        kernel,
        out_shape=out_shape,
        grid_spec=pltpu.PrefetchScalarGridSpec(
            num_scalar_prefetch=1, grid=grid, in_specs=in_specs, out_specs=out_specs, scratch_shapes=scratch
        ),
        input_output_aliases=aliases or {},
        compiler_params=pltpu.CompilerParams(vmem_limit_bytes=room * 1024 * 1024),
        cost_estimate=pl.CostEstimate(flops=0, bytes_accessed=1 << 12, transcendentals=0),
    )(scalars, *args)


def shape(*dims, dtype=f32):
    return jax.ShapeDtypeStruct(dims, dtype)


def swap(array, axis):
    return lax.ppermute(array, axis, [(0, 1), (1, 0)])


def flip(array, i):
    return lax.ppermute(array, NEAR, [(j, j ^ i) for j in range(4)])


def per_device(
    ssm_inputs,
    step_decay,
    state_inputs,
    state_readout,
    skip_gain,
    norm_gain,
    new_keys,
    new_values,
    cache_keys,
    cache_values,
    cache_len,
    out_weight,
):
    width = out_weight.shape[1] // 4
    core = lax.axis_index("c")
    near = lax.axis_index(NEAR)
    group = lax.axis_index(("yl", "za")).astype(jnp.int32)
    place = jnp.stack([lax.axis_index(CHIP), core, near, group]).astype(jnp.int32)
    of_group = lambda rows: pl.BlockSpec((1, rows, HD), lambda i, s: (s[3], 0, 0))

    piece = whole((2 * HD, width))
    filled, first, second = call(
        fill_kernel,
        place,
        (cache_keys, new_keys, cache_values, new_values, out_weight, out_weight),
        [of_group(CACHE), of_group(TOKENS), of_group(CACHE), of_group(TOKENS)]
        + [
            pl.BlockSpec((2 * HD, width), lambda i, s: (0, 2 * (s[2] // 2) + s[1])),
            pl.BlockSpec((2 * HD, width), lambda i, s: (0, 2 * (1 - s[2] // 2) + s[1])),
        ],
        (shape(CHIPS, ROWS, HD, dtype=bf16),) + (shape(2 * HD, width, dtype=bf16),) * 2,
        (pl.BlockSpec(memory_space=pl.ANY), piece, piece),
        scratch=[pltpu.VMEM((2 * SPAN, HD), bf16), pltpu.SemaphoreType.DMA((CHIPS,))],
        room=60,
    )
    place, filled = lax.optimization_barrier((place, filled))

    own = call(
        state_kernel,
        place,
        (ssm_inputs, step_decay, state_inputs),
        [whole((TOKENS, 2 * HD)), whole((4, TOKENS)), of_group(TOKENS)],
        shape(2, HD + 8, HD),
        whole((2, HD + 8, HD)),
    )
    both = lax.all_gather(own, "c")
    packed = call(
        pack_kernel,
        place,
        (both, cache_len, filled),
        [
            pl.BlockSpec((2, 1, HD + 8, HD), lambda i, s: (0, s[1], 0, 0)),
            SMEM,
            pl.BlockSpec(memory_space=pl.ANY),
        ],
        shape(CHIPS, ROWS, HD, dtype=bf16),
        pl.BlockSpec(memory_space=pl.ANY),
        scratch=[pltpu.VMEM((HEAD, HD), bf16), pltpu.SemaphoreType.DMA((CHIPS,))],
        room=60,
        aliases={3: 0},
    )

    second = flip(second, 2)
    third = flip(second, 1)
    same = lax.all_to_all(packed, CHIP, 0, 0, tiled=True)
    inside = call(
        inside_kernel,
        place,
        (ssm_inputs, step_decay, state_inputs, state_readout, skip_gain),
        [whole((TOKENS, 2 * HD)), whole((4, TOKENS)), of_group(TOKENS), of_group(TOKENS), SMEM],
        shape(2, TOKENS, HD),
        whole((2, TOKENS, HD)),
    )
    first = flip(first, 1)
    swapped = [swap(first, "c")]
    own_columns = lax.dynamic_slice_in_dim(out_weight, 2 * (near // 2) * width, 2 * width, 1)
    same, first, second, swapped, own_columns, inside = lax.optimization_barrier(
        (same, first, second, swapped, own_columns, inside)
    )
    other = swap(same, "c")
    entering = call(
        scan_kernel,
        place,
        (same,),
        [pl.BlockSpec((CHIPS, HEAD, HD), lambda i, s: (0, 0, 0))],
        shape(HD, HD),
        whole((HD, HD)),
    )
    carried = lax.all_gather(entering, "c")
    queries = call(
        query_kernel,
        place,
        (inside, step_decay, state_readout, carried, both, norm_gain.reshape(1, 2 * HD)),
        [
            whole((2, TOKENS, HD)),
            whole((4, TOKENS)),
            of_group(TOKENS),
            whole((2, HD, HD)),
            whole((2, 2, HD + 8, HD)),
            whole((1, 2 * HD)),
        ],
        shape(2 * TOKENS, HD, dtype=bf16),
        whole((2 * TOKENS, HD)),
    )

    attended = call(
        attend_kernel,
        place,
        (queries, same, other),
        [pl.BlockSpec(memory_space=pltpu.VMEM)] * 3,
        shape(4, TOKENS // 2, 2 * HD, dtype=bf16),
        whole((4, TOKENS // 2, 2 * HD)),
        scratch=[
            pltpu.VMEM((CHIPS, 2 * TOKENS, 2 * SPAN), f32),
            pltpu.VMEM((2 * TOKENS, HD), f32),
            pltpu.VMEM((2 * TOKENS, HD), f32),
            pltpu.VMEM((2 * TOKENS, HD), f32),
        ],
        room=24,
    )
    attended, second = lax.optimization_barrier((attended, second))
    received = (first, second, third)
    swapped = swapped + [swap(part, "c") for part in (second, third)]
    attended = lax.all_to_all(attended, NEAR, 0, 0, tiled=True)
    vmem = pl.BlockSpec(memory_space=pltpu.VMEM)
    keep, send = call(
        project_kernel,
        place,
        (attended, own_columns, *received, *swapped),
        [vmem] * 8,
        (shape(64, 2 * width, dtype=bf16),) * 2,
        (vmem,) * 2,
    )
    simple = functools.partial(pl.pallas_call, compiler_params=pltpu.CompilerParams(vmem_limit_bytes=40 * 1024 * 1024))
    partial = simple(add_kernel, out_shape=shape(64, 2 * width, dtype=bf16))(keep, swap(send, "yl"))
    parts = lax.all_to_all(partial.reshape(8, 8, 2 * width), OWNERS, 0, 0, tiled=True)
    return simple(finish_kernel, out_shape=shape(8, 4 * width, dtype=bf16))(parts)


def solution(mesh):
    fine = Mesh(mesh.devices.reshape(SIZES), AXES)
    placed = (
        P(PIPE, TENSOR),
        P(TENSOR, PIPE),
        P(None, PIPE, None),
        P(None, PIPE, None),
        P(TENSOR),
        P(TENSOR),
        P(None, PIPE, None),
        P(None, PIPE, None),
        P(None, PIPE, None),
        P(None, PIPE, None),
        P(PIPE),
        P(TENSOR, None),
    )
    return jax.shard_map(
        per_device,
        mesh=fine,
        in_specs=placed,
        out_specs=P(PIPE + TENSOR, None),
        check_vma=False,
    )
```

```python
import functools
import math

import jax
import jax.numpy as jnp
from jax import lax
from jax.experimental import pallas as pl
from jax.experimental.pallas import tpu as pltpu
from jax.sharding import Mesh
from jax.sharding import PartitionSpec as P

CACHE = 128
MH = 128
P_SIZE = 64
HD = 128
TOKENS = 256
SPAN = CACHE + TOKENS
TILE = 2 * HD + 16
HEAD = TILE + 16
ROWS = HEAD + 2 * SPAN
CHIPS = 8
HIDDEN = -1e30
SCALE = HD ** (-0.5) * math.log2(math.e)

AXES = ("x", "yh", "c", "yl", "za", "z1", "z0")
SIZES = (4, 2, 2, 2, 4, 2, 2)
PIPE = ("x", "yh", "c")
TENSOR = ("yl", "za", "z1", "z0")
CHIP = ("x", "yh")
NEAR = ("z1", "z0")
OWNERS = ("za", "z1")

bf16 = jnp.bfloat16
f32 = jnp.float32


def dot(a, b, contract=((1,), (0,))):
    return lax.dot_general(a, b, (contract, ((), ())), preferred_element_type=f32)


def thirds(value):
    high = value.astype(bf16)
    rest = value - high.astype(f32)
    middle = rest.astype(bf16)
    low = (rest - middle.astype(f32)).astype(bf16)
    return (low, middle, high)


def tri(transposed):
    first = lax.broadcasted_iota(jnp.int32, (TOKENS, TOKENS), 0)
    second = lax.broadcasted_iota(jnp.int32, (TOKENS, TOKENS), 1)
    return (first <= second) if transposed else (first >= second)


def cum_columns(decay):
    lower = tri(False).astype(f32).astype(bf16)
    return sum(dot(lower, part, ((1,), (1,))) for part in thirds(decay))


def cum_rows(decay):
    upper = tri(True).astype(f32).astype(bf16)
    return sum(dot(part, upper) for part in thirds(decay))


def low_lanes(rows):
    return lax.broadcasted_iota(jnp.int32, (rows, 2 * P_SIZE), 1) < P_SIZE


def spread(columns, half, rows):
    left, right = columns[:, 2 * half : 2 * half + 1], columns[:, 2 * half + 1 : 2 * half + 2]
    return jnp.where(low_lanes(rows), left, right)


def own_group():
    return lax.axis_index(("yl", "za"))


def state_kernel(x_ref, decay_ref, b_hbm, out_ref, b_ref, sem):
    copy = pltpu.make_async_copy(b_hbm.at[own_group()], b_ref, sem)
    copy.start()
    cum = cum_columns(decay_ref[...])
    last = cum[TOKENS - 1 :, :]
    tail = jnp.exp(last - cum)
    total = jnp.exp(-last)
    copy.wait()
    for half in range(2):
        inputs = x_ref[:, half * HD : (half + 1) * HD].astype(f32)
        weighted = (spread(tail, half, TOKENS) * inputs).astype(bf16)
        out_ref[half, 0:HD, :] = dot(b_ref[...], weighted, ((0,), (0,)))
        out_ref[half, HD : HD + 8, :] = spread(jnp.broadcast_to(total, (8, 4)), half, 8)


def spread_copies(held, out_ref, begin, sems):
    rows = held.shape[0]
    copies = [pltpu.make_async_copy(held, out_ref.at[k, begin : begin + rows], sems.at[k]) for k in range(CHIPS)]
    for copy in copies:
        copy.start()
    for copy in copies:
        copy.wait()


def spread_copies(held, out_ref, begin, sems):
    rows = held.shape[0]
    copies = [pltpu.make_async_copy(held, out_ref.at[k, begin : begin + rows], sems.at[k]) for k in range(CHIPS)]
    for copy in copies:
        copy.start()
    return copies


def fill_kernel(ck_ref, nk_ref, cv_ref, nv_ref, w_ref, len_hbm, out_ref, *refs):
    w_outs, (held, w_held, len_ref, in_sems, w_sems, sems) = refs[:2], refs[2:]
    core, side, group = lax.axis_index("c"), lax.axis_index("z1"), own_group()
    width = w_held.shape[2]
    loads, begin = [], HEAD - TILE
    for i, ref in enumerate((ck_ref, nk_ref, cv_ref, nv_ref)):
        rows = ref.shape[1]
        loads.append(pltpu.make_async_copy(ref.at[group], held.at[begin : begin + rows], in_sems.at[i]))
        begin = begin + rows
    pieces = []
    for i, half in enumerate((side, 1 - side)):
        columns = pl.ds(pl.multiple_of((2 * half + core) * width, width), width)
        pieces.append(pltpu.make_async_copy(w_ref.at[:, columns], w_held.at[i], in_sems.at[4 + i]))
    loads.append(pltpu.make_async_copy(len_hbm, len_ref, in_sems.at[6]))
    for copy in loads + pieces:
        copy.start()
    loads.pop().wait()
    slots = lax.broadcasted_iota(jnp.int32, (HEAD - TILE, HD), 1)
    held[0 : HEAD - TILE, :] = jnp.where(slots < len_ref[0], 0.0, HIDDEN).astype(bf16)
    for copy in loads:
        copy.wait()
    copies = spread_copies(held, out_ref, TILE, sems)
    for i, copy in enumerate(pieces):
        copy.wait()
        copies.append(pltpu.make_async_copy(w_held.at[i], w_outs[i], w_sems.at[i]))
        copies[-1].start()
    for copy in copies:
        copy.wait()


def pack_kernel(both_ref, filled_ref, out_ref, held, sems):
    core = lax.axis_index("c")
    first, second = both_ref[0, core], both_ref[1, core]
    state = first[0:HD] * second[HD : HD + 1] + second[0:HD]
    high = state.astype(bf16)
    held[0:HD, :] = high
    held[HD : 2 * HD, :] = (state - high.astype(f32)).astype(bf16)
    row = lax.broadcasted_iota(jnp.int32, (TILE - 2 * HD, HD), 0)
    tile = jnp.zeros((TILE - 2 * HD, HD), f32)
    for i, part in enumerate(thirds(first[HD : HD + 1] * second[HD : HD + 1])):
        tile = jnp.where(row == i, part.astype(f32), tile)
    held[2 * HD : TILE, :] = tile.astype(bf16)
    for copy in spread_copies(held, out_ref, 0, sems):
        copy.wait()


def scan_kernel(place_ref, all_ref, out_ref):
    chip = place_ref[0]
    state = jnp.zeros((HD, HD), f32)
    for k in range(CHIPS - 1):
        tile = all_ref[k, 2 * HD : TILE, :].astype(f32)
        decay = tile[0:1] + tile[1:2] + tile[2:3]
        here = all_ref[k, 0:HD, :].astype(f32) + all_ref[k, HD : 2 * HD, :].astype(f32)
        state = jnp.where(k < chip, decay * state + here, state)
    out_ref[...] = state


def inside_kernel(group_ref, x_ref, decay_ref, b_ref, c_ref, gain_ref, y_ref):
    decay = decay_ref[...]
    columns, rows = cum_columns(decay), cum_rows(decay)
    causal = tri(False)
    gram = dot(c_ref[0], b_ref[0], ((1,), (1,)))
    for half in range(2):
        inputs = x_ref[:, half * HD : (half + 1) * HD]
        pieces = []
        for head in (2 * half, 2 * half + 1):
            diff = jnp.where(causal, columns[:, head : head + 1] - rows[head : head + 1, :], 0.0)
            weights = jnp.where(causal, gram * jnp.exp(-diff), 0.0).astype(bf16)
            pieces.append(dot(weights, inputs))
        low = low_lanes(TOKENS)
        skip = jnp.where(low_lanes(1), gain_ref[2 * half], gain_ref[2 * half + 1])
        y_ref[half] = jnp.where(low, pieces[0], pieces[1]) + skip * inputs.astype(f32)


def query_kernel(place_ref, y_ref, decay_ref, c_ref, carried_ref, both_ref, gain_ref, out_ref):
    core = place_ref[1]
    readout = c_ref[0]
    low = low_lanes(TOKENS)
    fade = jnp.exp(-cum_columns(decay_ref[...]))
    for half in range(2):
        carried = carried_ref[half]
        after = both_ref[0, half, HD : HD + 1] * carried + both_ref[0, half, 0:HD]
        carried = jnp.where(core == 1, after, carried)
        from_state = sum(dot(readout, part) for part in thirds(carried))
        y = y_ref[half] + spread(fade, half, TOKENS) * from_state
        square = y * y
        left = jnp.sum(jnp.where(low, square, 0.0), axis=1, keepdims=True)
        right = jnp.sum(jnp.where(low, 0.0, square), axis=1, keepdims=True)
        mean = jnp.where(low, left, right) * (1.0 / P_SIZE)
        normed = y * lax.rsqrt(mean + 1e-05) * gain_ref[0:1, half * HD : (half + 1) * HD]
        out_ref[half * TOKENS : (half + 1) * TOKENS, :] = normed.astype(bf16)


def attend_kernel(place_ref, q_ref, a_ref, b_ref, out_ref, scores_ref, top_ref, sum_ref, acc_ref):
    chip, core = place_ref[0], place_ref[1]
    count = q_ref.shape[0]
    sides = (a_ref, b_ref)
    top_ref[...] = jnp.full((count, HD), -jnp.inf, f32)

    def score(k, side, extra, causal):
        bias = sides[side][k, TILE:HEAD, :].astype(f32)[0:1]
        raw = dot(q_ref[...], sides[side][k, HEAD : HEAD + SPAN, :], ((1,), (1,))) * SCALE
        top = top_ref[...]
        for tile in range(SPAN // HD):
            part = raw[:, tile * HD : (tile + 1) * HD]
            if tile == 0:
                part = part + (bias if extra is None else bias + extra)
            elif causal:
                token = lax.broadcasted_iota(jnp.int32, (count, HD), 0) % TOKENS
                key = lax.broadcasted_iota(jnp.int32, (count, HD), 1) + (tile - 1) * HD
                part = jnp.where(key <= token, part, HIDDEN)
            elif extra is not None:
                part = part + extra
            top = jnp.maximum(top, part)
            scores_ref[k, :, side * SPAN + tile * HD : side * SPAN + (tile + 1) * HD] = part
        top_ref[...] = top

    def early(k, carry):
        score(k, 0, None, False)
        score(k, 1, None, False)
        return carry

    lax.fori_loop(0, chip, early, 0)
    score(chip, 0, None, True)
    score(chip, 1, jnp.where(core == 1, 0.0, HIDDEN), False)

    top = jnp.max(top_ref[...], axis=1, keepdims=True)
    top_ref[...] = jnp.broadcast_to(top, (count, HD))
    sum_ref[...] = jnp.zeros((count, HD), f32)
    acc_ref[...] = jnp.zeros((count, HD), f32)

    def late(k, carry):
        top = top_ref[...]
        total = sum_ref[...]
        acc = acc_ref[...]
        for side in range(2):
            probs = []
            for tile in range(SPAN // HD):
                part = scores_ref[k, :, side * SPAN + tile * HD : side * SPAN + (tile + 1) * HD]
                expo = jnp.exp2(part - top)
                total = total + expo
                probs.append(expo.astype(bf16))
            acc = acc + dot(jnp.concatenate(probs, axis=1), sides[side][k, HEAD + SPAN :, :])
        sum_ref[...] = total
        acc_ref[...] = acc
        return carry

    lax.fori_loop(0, chip + 1, late, 0)
    total = jnp.sum(sum_ref[...], axis=1, keepdims=True)
    result = acc_ref[...] / total
    for z0 in range(2):
        for half in range(2):
            blocks = [16 * yl + 4 * za + 2 * z1 + z0 for yl in range(2) for za in range(4) for z1 in range(2)]
            rows = [half * TOKENS + 8 * block for block in blocks]
            piece = jnp.concatenate([result[row : row + 8] for row in rows], axis=0).astype(bf16)
            for z1 in range(2):
                out_ref[2 * z1 + z0, :, half * HD : (half + 1) * HD] = piece


def project_kernel(place_ref, att_ref, own_ref, r1, r2, r3, s1, s2, s3, keep_ref, send_ref):
    near, core, side = place_ref[2], place_ref[1], place_ref[3] // 4
    rows, width = keep_ref.shape[0], r1.shape[1]

    def run(others, begin):
        total = dot(att_ref[near], own_ref[:, begin : begin + width])
        for i, ref in enumerate(others):
            total = total + dot(att_ref[near ^ (i + 1)], ref[...])
        total = total.astype(bf16)

        @pl.when(side == 0)
        def _():
            keep_ref[:, begin : begin + width] = total[:rows]
            send_ref[:, begin : begin + width] = total[rows:]

        @pl.when(side == 1)
        def _():
            keep_ref[:, begin : begin + width] = total[rows:]
            send_ref[:, begin : begin + width] = total[:rows]

    @pl.when(core == 0)
    def _():
        run((r1, r2, r3), 0)
        run((s1, s2, s3), width)

    @pl.when(core == 1)
    def _():
        run((s1, s2, s3), 0)
        run((r1, r2, r3), width)


def add_kernel(first_ref, second_ref, out_ref):
    out_ref[...] = (first_ref[...].astype(f32) + second_ref[...].astype(f32)).astype(bf16)


def finish_kernel(parts_ref, out_ref):
    for half in range(2):
        total = parts_ref[half].astype(f32)
        for i in range(1, 4):
            total = total + parts_ref[2 * i + half].astype(f32)
        width = parts_ref.shape[2]
        out_ref[:, half * width : (half + 1) * width] = total.astype(bf16)


def whole(shape):
    return pl.BlockSpec(shape, lambda *_: (0,) * len(shape))


SMEM = pl.BlockSpec(memory_space=pltpu.SMEM)


def call(kernel, scalars, args, in_specs, out_shape, out_specs, grid=(1,), scratch=(), room=16, aliases=None):
    return pl.pallas_call(
        kernel,
        out_shape=out_shape,
        grid_spec=pltpu.PrefetchScalarGridSpec(
            num_scalar_prefetch=1, grid=grid, in_specs=in_specs, out_specs=out_specs, scratch_shapes=scratch
        ),
        input_output_aliases=aliases or {},
        compiler_params=pltpu.CompilerParams(vmem_limit_bytes=room * 1024 * 1024),
        cost_estimate=pl.CostEstimate(flops=0, bytes_accessed=1 << 12, transcendentals=0),
    )(scalars, *args)


def plain(kernel, args, in_specs, out_shape, out_specs, scratch, aliases=None):
    return pl.pallas_call(
        kernel,
        out_shape=out_shape,
        in_specs=in_specs,
        out_specs=out_specs,
        scratch_shapes=scratch,
        input_output_aliases=aliases or {},
        compiler_params=pltpu.CompilerParams(vmem_limit_bytes=60 * 1024 * 1024),
        cost_estimate=pl.CostEstimate(flops=0, bytes_accessed=1 << 12, transcendentals=0),
    )(*args)


def shape(*dims, dtype=f32):
    return jax.ShapeDtypeStruct(dims, dtype)


def swap(array, axis):
    return lax.ppermute(array, axis, [(0, 1), (1, 0)])


def flip(array, i):
    return lax.ppermute(array, NEAR, [(j, j ^ i) for j in range(4)])


def per_device(
    ssm_inputs,
    step_decay,
    state_inputs,
    state_readout,
    skip_gain,
    norm_gain,
    new_keys,
    new_values,
    cache_keys,
    cache_values,
    cache_len,
    out_weight,
):
    width = out_weight.shape[1] // 4
    core = lax.axis_index("c")
    near = lax.axis_index(NEAR)
    group = lax.axis_index(("yl", "za")).astype(jnp.int32)
    of_group = lambda rows: pl.BlockSpec((1, rows, HD), lambda i, s: (s[3], 0, 0))

    hbm = pl.BlockSpec(memory_space=pltpu.HBM)
    vmem = pl.BlockSpec(memory_space=pltpu.VMEM)
    filled, first, second = plain(
        fill_kernel,
        (cache_keys, new_keys, cache_values, new_values, out_weight, cache_len),
        [hbm] * 6,
        (shape(CHIPS, ROWS, HD, dtype=bf16),) + (shape(2 * HD, width, dtype=bf16),) * 2,
        (hbm,) * 3,
        [
            pltpu.VMEM((ROWS - TILE, HD), bf16),
            pltpu.VMEM((2, 2 * HD, width), bf16),
            pltpu.SMEM((1,), jnp.int32),
            pltpu.SemaphoreType.DMA((7,)),
            pltpu.SemaphoreType.DMA((2,)),
            pltpu.SemaphoreType.DMA((CHIPS,)),
        ],
    )
    step_decay, filled = lax.optimization_barrier((step_decay, filled))

    own = pl.pallas_call(
        state_kernel,
        out_shape=shape(2, HD + 8, HD),
        in_specs=[vmem, vmem, hbm],
        out_specs=vmem,
        scratch_shapes=[pltpu.VMEM((TOKENS, HD), bf16), pltpu.SemaphoreType.DMA],
        compiler_params=pltpu.CompilerParams(vmem_limit_bytes=16 * 1024 * 1024),
        cost_estimate=pl.CostEstimate(flops=0, bytes_accessed=1 << 12, transcendentals=0),
    )(ssm_inputs, step_decay, state_inputs)
    both = lax.all_gather(own, "c")
    packed = plain(
        pack_kernel,
        (both, filled),
        [vmem, hbm],
        shape(CHIPS, ROWS, HD, dtype=bf16),
        hbm,
        [pltpu.VMEM((TILE, HD), bf16), pltpu.SemaphoreType.DMA((CHIPS,))],
        {1: 0},
    )
    place = jnp.stack([lax.axis_index(CHIP), core, near, group]).astype(jnp.int32)
    second = flip(second, 2)
    third = flip(second, 1)
    same = lax.all_to_all(packed, CHIP, 0, 0, tiled=True)
    inside = call(
        inside_kernel,
        place,
        (ssm_inputs, step_decay, state_inputs, state_readout, skip_gain),
        [whole((TOKENS, 2 * HD)), whole((4, TOKENS)), of_group(TOKENS), of_group(TOKENS), SMEM],
        shape(2, TOKENS, HD),
        whole((2, TOKENS, HD)),
    )
    first = flip(first, 1)
    own_columns = lax.dynamic_slice_in_dim(out_weight, 2 * (near // 2) * width, 2 * width, 1)
    first, inside = lax.optimization_barrier((first, inside))
    swapped = [swap(first, "c")]
    same, second, swapped, own_columns = lax.optimization_barrier((same, second, swapped, own_columns))
    other = swap(same, "c")
    entering = call(
        scan_kernel,
        place,
        (same,),
        [pl.BlockSpec((CHIPS, TILE, HD), lambda i, s: (0, 0, 0))],
        shape(HD, HD),
        whole((HD, HD)),
    )
    carried = lax.all_gather(entering, "c")
    queries = call(
        query_kernel,
        place,
        (inside, step_decay, state_readout, carried, both, norm_gain.reshape(1, 2 * HD)),
        [
            whole((2, TOKENS, HD)),
            whole((4, TOKENS)),
            of_group(TOKENS),
            whole((2, HD, HD)),
            whole((2, 2, HD + 8, HD)),
            whole((1, 2 * HD)),
        ],
        shape(2 * TOKENS, HD, dtype=bf16),
        whole((2 * TOKENS, HD)),
    )

    attended = call(
        attend_kernel,
        place,
        (queries, same, other),
        [pl.BlockSpec(memory_space=pltpu.VMEM)] * 3,
        shape(4, TOKENS // 2, 2 * HD, dtype=bf16),
        whole((4, TOKENS // 2, 2 * HD)),
        scratch=[
            pltpu.VMEM((CHIPS, 2 * TOKENS, 2 * SPAN), f32),
            pltpu.VMEM((2 * TOKENS, HD), f32),
            pltpu.VMEM((2 * TOKENS, HD), f32),
            pltpu.VMEM((2 * TOKENS, HD), f32),
        ],
        room=24,
    )
    attended, second = lax.optimization_barrier((attended, second))
    received = (first, second, third)
    swapped = swapped + [swap(part, "c") for part in (second, third)]
    attended = lax.all_to_all(attended, NEAR, 0, 0, tiled=True)
    vmem = pl.BlockSpec(memory_space=pltpu.VMEM)
    keep, send = call(
        project_kernel,
        place,
        (attended, own_columns, *received, *swapped),
        [vmem] * 8,
        (shape(64, 2 * width, dtype=bf16),) * 2,
        (vmem,) * 2,
    )
    simple = functools.partial(pl.pallas_call, compiler_params=pltpu.CompilerParams(vmem_limit_bytes=40 * 1024 * 1024))
    partial = simple(add_kernel, out_shape=shape(64, 2 * width, dtype=bf16))(keep, swap(send, "yl"))
    parts = lax.all_to_all(partial.reshape(8, 8, 2 * width), OWNERS, 0, 0, tiled=True)
    return simple(finish_kernel, out_shape=shape(8, 4 * width, dtype=bf16))(parts)


def solution(mesh):
    fine = Mesh(mesh.devices.reshape(SIZES), AXES)
    placed = (
        P(PIPE, TENSOR),
        P(TENSOR, PIPE),
        P(None, PIPE, None),
        P(None, PIPE, None),
        P(TENSOR),
        P(TENSOR),
        P(None, PIPE, None),
        P(None, PIPE, None),
        P(None, PIPE, None),
        P(None, PIPE, None),
        P(PIPE),
        P(TENSOR, None),
    )
    return jax.shard_map(
        per_device,
        mesh=fine,
        in_specs=placed,
        out_specs=P(PIPE + TENSOR, None),
        check_vma=False,
    )
```

```python
import functools
import math

import jax
import jax.numpy as jnp
from jax import lax
from jax.experimental import pallas as pl
from jax.experimental.pallas import tpu as pltpu
from jax.sharding import Mesh
from jax.sharding import PartitionSpec as P

CACHE = 128
MH = 128
P_SIZE = 64
HD = 128
TOKENS = 256
SPAN = CACHE + TOKENS
TILE = 2 * HD + 16
HEAD = TILE + 16
ROWS = HEAD + 2 * SPAN
CHIPS = 8
HIDDEN = -1e30
SCALE = HD ** (-0.5) * math.log2(math.e)

AXES = ("x", "yh", "c", "yl", "za", "z1", "z0")
SIZES = (4, 2, 2, 2, 4, 2, 2)
PIPE = ("x", "yh", "c")
TENSOR = ("yl", "za", "z1", "z0")
CHIP = ("x", "yh")
BLOCKS = ("yh", "x")
NEAR = ("z1", "z0")
OWNERS = ("za", "z1")

bf16 = jnp.bfloat16
f32 = jnp.float32


def dot(a, b, contract=((1,), (0,))):
    return lax.dot_general(a, b, (contract, ((), ())), preferred_element_type=f32)


def thirds(value):
    high = value.astype(bf16)
    rest = value - high.astype(f32)
    middle = rest.astype(bf16)
    low = (rest - middle.astype(f32)).astype(bf16)
    return (low, middle, high)


def tri(transposed):
    first = lax.broadcasted_iota(jnp.int32, (TOKENS, TOKENS), 0)
    second = lax.broadcasted_iota(jnp.int32, (TOKENS, TOKENS), 1)
    return (first <= second) if transposed else (first >= second)


def cum_columns(decay):
    lower = tri(False).astype(f32).astype(bf16)
    return sum(dot(lower, part, ((1,), (1,))) for part in thirds(decay))


def cum_rows(decay):
    upper = tri(True).astype(f32).astype(bf16)
    return sum(dot(part, upper) for part in thirds(decay))


def low_lanes(rows):
    return lax.broadcasted_iota(jnp.int32, (rows, 2 * P_SIZE), 1) < P_SIZE


def spread(columns, half, rows):
    left, right = columns[:, 2 * half : 2 * half + 1], columns[:, 2 * half + 1 : 2 * half + 2]
    return jnp.where(low_lanes(rows), left, right)


def own_group():
    return lax.axis_index(("yl", "za"))


def state_kernel(x_ref, decay_ref, b_hbm, out_ref, b_ref, sem):
    copy = pltpu.make_async_copy(b_hbm.at[own_group()], b_ref, sem)
    copy.start()
    cum = cum_columns(decay_ref[...])
    last = cum[TOKENS - 1 :, :]
    tail = jnp.exp(last - cum)
    total = jnp.exp(-last)
    copy.wait()
    for half in range(2):
        inputs = x_ref[:, half * HD : (half + 1) * HD].astype(f32)
        weighted = (spread(tail, half, TOKENS) * inputs).astype(bf16)
        out_ref[half, 0:HD, :] = dot(b_ref[...], weighted, ((0,), (0,)))
        out_ref[half, HD : HD + 8, :] = spread(jnp.broadcast_to(total, (8, 4)), half, 8)


def block_of(chip):
    return 4 * (chip % 2) + chip // 2


def spread_copies(held, out_ref, begin, sems):
    rows = held.shape[0]
    copies = [pltpu.make_async_copy(held, out_ref.at[k, begin : begin + rows], sems.at[k]) for k in range(CHIPS)]
    for copy in copies:
        copy.start()
    for copy in copies:
        copy.wait()


def block_of(chip):
    return 4 * (chip % 2) + chip // 2


def spread_copies(held, out_ref, begin, sems):
    rows = held.shape[0]
    copies = [pltpu.make_async_copy(held, out_ref.at[k, begin : begin + rows], sems.at[k]) for k in range(CHIPS)]
    for copy in copies:
        copy.start()
    return copies


def fill_kernel(ck_ref, nk_ref, cv_ref, nv_ref, w_ref, len_hbm, out_ref, *refs):
    w_outs, (held, w_held, len_ref, in_sems, w_sems, sems) = refs[:2], refs[2:]
    core, side, group = lax.axis_index("c"), lax.axis_index("z1"), own_group()
    width = w_held.shape[2]
    loads, begin = [], HEAD - TILE
    for i, ref in enumerate((ck_ref, nk_ref, cv_ref, nv_ref)):
        rows = ref.shape[1]
        loads.append(pltpu.make_async_copy(ref.at[group], held.at[begin : begin + rows], in_sems.at[i]))
        begin = begin + rows
    pieces = []
    for i, half in enumerate((side, 1 - side)):
        columns = pl.ds(pl.multiple_of((2 * half + core) * width, width), width)
        pieces.append(pltpu.make_async_copy(w_ref.at[:, columns], w_held.at[i], in_sems.at[4 + i]))
    loads.append(pltpu.make_async_copy(len_hbm, len_ref, in_sems.at[6]))
    for copy in loads + pieces:
        copy.start()
    loads.pop().wait()
    slots = lax.broadcasted_iota(jnp.int32, (HEAD - TILE, HD), 1)
    held[0 : HEAD - TILE, :] = jnp.where(slots < len_ref[0], 0.0, HIDDEN).astype(bf16)
    for copy in loads:
        copy.wait()
    copies = spread_copies(held, out_ref, TILE, sems)
    for i, copy in enumerate(pieces):
        copy.wait()
        copies.append(pltpu.make_async_copy(w_held.at[i], w_outs[i], w_sems.at[i]))
        copies[-1].start()
    for copy in copies:
        copy.wait()


def pack_kernel(both_ref, filled_ref, out_ref, held, sems):
    core = lax.axis_index("c")
    first, second = both_ref[0, core], both_ref[1, core]
    state = first[0:HD] * second[HD : HD + 1] + second[0:HD]
    high = state.astype(bf16)
    held[0:HD, :] = high
    held[HD : 2 * HD, :] = (state - high.astype(f32)).astype(bf16)
    row = lax.broadcasted_iota(jnp.int32, (TILE - 2 * HD, HD), 0)
    tile = jnp.zeros((TILE - 2 * HD, HD), f32)
    for i, part in enumerate(thirds(first[HD : HD + 1] * second[HD : HD + 1])):
        tile = jnp.where(row == i, part.astype(f32), tile)
    held[2 * HD : TILE, :] = tile.astype(bf16)
    for copy in spread_copies(held, out_ref, 0, sems):
        copy.wait()


def scan_kernel(all_ref, out_ref):
    chip = lax.axis_index(CHIP)
    state = jnp.zeros((HD, HD), f32)
    for k in range(CHIPS - 1):
        block = block_of(k)
        tile = all_ref[block, 2 * HD : TILE, :].astype(f32)
        decay = tile[0:1] + tile[1:2] + tile[2:3]
        here = all_ref[block, 0:HD, :].astype(f32) + all_ref[block, HD : 2 * HD, :].astype(f32)
        state = jnp.where(k < chip, decay * state + here, state)
    out_ref[...] = state


def inside_kernel(group_ref, x_ref, decay_ref, b_ref, c_ref, gain_ref, y_ref):
    decay = decay_ref[...]
    columns, rows = cum_columns(decay), cum_rows(decay)
    causal = tri(False)
    gram = dot(c_ref[0], b_ref[0], ((1,), (1,)))
    for half in range(2):
        inputs = x_ref[:, half * HD : (half + 1) * HD]
        pieces = []
        for head in (2 * half, 2 * half + 1):
            diff = jnp.where(causal, columns[:, head : head + 1] - rows[head : head + 1, :], 0.0)
            weights = jnp.where(causal, gram * jnp.exp(-diff), 0.0).astype(bf16)
            pieces.append(dot(weights, inputs))
        low = low_lanes(TOKENS)
        skip = jnp.where(low_lanes(1), gain_ref[2 * half], gain_ref[2 * half + 1])
        y_ref[half] = jnp.where(low, pieces[0], pieces[1]) + skip * inputs.astype(f32)


def query_kernel(y_ref, decay_ref, c_hbm, carried_ref, both_ref, gain_ref, out_ref, c_ref, sem):
    core = lax.axis_index("c")
    copy = pltpu.make_async_copy(c_hbm.at[own_group()], c_ref, sem)
    copy.start()
    low = low_lanes(TOKENS)
    fade = jnp.exp(-cum_columns(decay_ref[...]))
    copy.wait()
    readout = c_ref[...]
    for half in range(2):
        carried = carried_ref[half]
        after = both_ref[0, half, HD : HD + 1] * carried + both_ref[0, half, 0:HD]
        carried = jnp.where(core == 1, after, carried)
        from_state = sum(dot(readout, part) for part in thirds(carried))
        y = y_ref[half] + spread(fade, half, TOKENS) * from_state
        square = y * y
        left = jnp.sum(jnp.where(low, square, 0.0), axis=1, keepdims=True)
        right = jnp.sum(jnp.where(low, 0.0, square), axis=1, keepdims=True)
        mean = jnp.where(low, left, right) * (1.0 / P_SIZE)
        normed = y * lax.rsqrt(mean + 1e-05) * gain_ref[0:1, half * HD : (half + 1) * HD]
        out_ref[half * TOKENS : (half + 1) * TOKENS, :] = normed.astype(bf16)


def attend_kernel(q_ref, a_ref, b_ref, out_ref, scores_ref, top_ref, sum_ref, acc_ref):
    chip, core = lax.axis_index(CHIP), lax.axis_index("c")
    count = q_ref.shape[0]
    sides = (a_ref, b_ref)
    top_ref[...] = jnp.full((count, HD), -jnp.inf, f32)

    def score(k, side, extra, causal):
        bias = sides[side][block_of(k), TILE:HEAD, :].astype(f32)[0:1]
        raw = dot(q_ref[...], sides[side][block_of(k), HEAD : HEAD + SPAN, :], ((1,), (1,))) * SCALE
        top = top_ref[...]
        for tile in range(SPAN // HD):
            part = raw[:, tile * HD : (tile + 1) * HD]
            if tile == 0:
                part = part + (bias if extra is None else bias + extra)
            elif causal:
                token = lax.broadcasted_iota(jnp.int32, (count, HD), 0) % TOKENS
                key = lax.broadcasted_iota(jnp.int32, (count, HD), 1) + (tile - 1) * HD
                part = jnp.where(key <= token, part, HIDDEN)
            elif extra is not None:
                part = part + extra
            top = jnp.maximum(top, part)
            scores_ref[k, :, side * SPAN + tile * HD : side * SPAN + (tile + 1) * HD] = part
        top_ref[...] = top

    def early(k, carry):
        score(k, 0, None, False)
        score(k, 1, None, False)
        return carry

    lax.fori_loop(0, chip, early, 0)
    score(chip, 0, None, True)
    score(chip, 1, jnp.where(core == 1, 0.0, HIDDEN), False)

    top = jnp.max(top_ref[...], axis=1, keepdims=True)
    top_ref[...] = jnp.broadcast_to(top, (count, HD))
    sum_ref[...] = jnp.zeros((count, HD), f32)
    acc_ref[...] = jnp.zeros((count, HD), f32)

    def late(k, carry):
        top = top_ref[...]
        total = sum_ref[...]
        acc = acc_ref[...]
        for side in range(2):
            probs = []
            for tile in range(SPAN // HD):
                part = scores_ref[k, :, side * SPAN + tile * HD : side * SPAN + (tile + 1) * HD]
                expo = jnp.exp2(part - top)
                total = total + expo
                probs.append(expo.astype(bf16))
            acc = acc + dot(jnp.concatenate(probs, axis=1), sides[side][block_of(k), HEAD + SPAN :, :])
        sum_ref[...] = total
        acc_ref[...] = acc
        return carry

    lax.fori_loop(0, chip + 1, late, 0)
    total = jnp.sum(sum_ref[...], axis=1, keepdims=True)
    result = acc_ref[...] / total
    for z0 in range(2):
        for half in range(2):
            blocks = [16 * yl + 4 * za + 2 * z1 + z0 for yl in range(2) for za in range(4) for z1 in range(2)]
            rows = [half * TOKENS + 8 * block for block in blocks]
            piece = jnp.concatenate([result[row : row + 8] for row in rows], axis=0).astype(bf16)
            for z1 in range(2):
                out_ref[2 * z1 + z0, :, half * HD : (half + 1) * HD] = piece


def project_kernel(att_ref, own_ref, r1, r2, r3, s1, s2, s3, keep_ref, send_ref):
    near, core, side = lax.axis_index(NEAR), lax.axis_index("c"), lax.axis_index("yl")
    rows, width = keep_ref.shape[0], r1.shape[1]

    def run(others, begin):
        total = dot(att_ref[near], own_ref[:, begin : begin + width])
        for i, ref in enumerate(others):
            total = total + dot(att_ref[near ^ (i + 1)], ref[...])
        total = total.astype(bf16)

        @pl.when(side == 0)
        def _():
            keep_ref[:, begin : begin + width] = total[:rows]
            send_ref[:, begin : begin + width] = total[rows:]

        @pl.when(side == 1)
        def _():
            keep_ref[:, begin : begin + width] = total[rows:]
            send_ref[:, begin : begin + width] = total[:rows]

    @pl.when(core == 0)
    def _():
        run((r1, r2, r3), 0)
        run((s1, s2, s3), width)

    @pl.when(core == 1)
    def _():
        run((s1, s2, s3), 0)
        run((r1, r2, r3), width)


def add_kernel(first_ref, second_ref, out_ref):
    out_ref[...] = (first_ref[...].astype(f32) + second_ref[...].astype(f32)).astype(bf16)


def finish_kernel(parts_ref, out_ref):
    for half in range(2):
        total = parts_ref[half].astype(f32)
        for i in range(1, 4):
            total = total + parts_ref[2 * i + half].astype(f32)
        width = parts_ref.shape[2]
        out_ref[:, half * width : (half + 1) * width] = total.astype(bf16)


def whole(shape):
    return pl.BlockSpec(shape, lambda *_: (0,) * len(shape))


SMEM = pl.BlockSpec(memory_space=pltpu.SMEM)


def call(kernel, scalars, args, in_specs, out_shape, out_specs, grid=(1,), scratch=(), room=16, aliases=None):
    return pl.pallas_call(
        kernel,
        out_shape=out_shape,
        grid_spec=pltpu.PrefetchScalarGridSpec(
            num_scalar_prefetch=1, grid=grid, in_specs=in_specs, out_specs=out_specs, scratch_shapes=scratch
        ),
        input_output_aliases=aliases or {},
        compiler_params=pltpu.CompilerParams(vmem_limit_bytes=room * 1024 * 1024),
        cost_estimate=pl.CostEstimate(flops=0, bytes_accessed=1 << 12, transcendentals=0),
    )(scalars, *args)


def plain(kernel, args, in_specs, out_shape, out_specs, scratch=(), aliases=None, room=16):
    return pl.pallas_call(
        kernel,
        out_shape=out_shape,
        in_specs=in_specs,
        out_specs=out_specs,
        scratch_shapes=scratch,
        input_output_aliases=aliases or {},
        compiler_params=pltpu.CompilerParams(vmem_limit_bytes=room * 1024 * 1024),
        cost_estimate=pl.CostEstimate(flops=0, bytes_accessed=1 << 12, transcendentals=0),
    )(*args)


def shape(*dims, dtype=f32):
    return jax.ShapeDtypeStruct(dims, dtype)


def swap(array, axis):
    return lax.ppermute(array, axis, [(0, 1), (1, 0)])


def flip(array, i):
    return lax.ppermute(array, NEAR, [(j, j ^ i) for j in range(4)])


def per_device(
    ssm_inputs,
    step_decay,
    state_inputs,
    state_readout,
    skip_gain,
    norm_gain,
    new_keys,
    new_values,
    cache_keys,
    cache_values,
    cache_len,
    out_weight,
):
    width = out_weight.shape[1] // 4
    core = lax.axis_index("c")
    near = lax.axis_index(NEAR)
    group = lax.axis_index(("yl", "za")).astype(jnp.int32)
    of_group = lambda rows: pl.BlockSpec((1, rows, HD), lambda i, s: (s[3], 0, 0))

    hbm = pl.BlockSpec(memory_space=pltpu.HBM)
    vmem = pl.BlockSpec(memory_space=pltpu.VMEM)
    filled, first, second = plain(
        fill_kernel,
        (cache_keys, new_keys, cache_values, new_values, out_weight, cache_len),
        [hbm] * 6,
        (shape(CHIPS, ROWS, HD, dtype=bf16),) + (shape(2 * HD, width, dtype=bf16),) * 2,
        (hbm,) * 3,
        [
            pltpu.VMEM((ROWS - TILE, HD), bf16),
            pltpu.VMEM((2, 2 * HD, width), bf16),
            pltpu.SMEM((1,), jnp.int32),
            pltpu.SemaphoreType.DMA((7,)),
            pltpu.SemaphoreType.DMA((2,)),
            pltpu.SemaphoreType.DMA((CHIPS,)),
        ],
        room=60,
    )
    step_decay, filled = lax.optimization_barrier((step_decay, filled))

    own = plain(
        state_kernel,
        (ssm_inputs, step_decay, state_inputs),
        [vmem, vmem, hbm],
        shape(2, HD + 8, HD),
        vmem,
        [pltpu.VMEM((TOKENS, HD), bf16), pltpu.SemaphoreType.DMA],
    )
    both = lax.all_gather(own, "c")
    packed = plain(
        pack_kernel,
        (both, filled),
        [vmem, hbm],
        shape(CHIPS, ROWS, HD, dtype=bf16),
        hbm,
        [pltpu.VMEM((TILE, HD), bf16), pltpu.SemaphoreType.DMA((CHIPS,))],
        {1: 0},
        room=60,
    )
    place = jnp.stack([lax.axis_index(CHIP), core, near, group]).astype(jnp.int32)
    second = flip(second, 2)
    third = flip(second, 1)
    same = lax.all_to_all(packed, BLOCKS, 0, 0, tiled=True)
    inside = call(
        inside_kernel,
        place,
        (ssm_inputs, step_decay, state_inputs, state_readout, skip_gain),
        [whole((TOKENS, 2 * HD)), whole((4, TOKENS)), of_group(TOKENS), of_group(TOKENS), SMEM],
        shape(2, TOKENS, HD),
        whole((2, TOKENS, HD)),
    )
    first = flip(first, 1)
    own_columns = lax.dynamic_slice_in_dim(out_weight, 2 * (near // 2) * width, 2 * width, 1)
    first, inside = lax.optimization_barrier((first, inside))
    swapped = [swap(first, "c")]
    same, second, swapped, own_columns = lax.optimization_barrier((same, second, swapped, own_columns))
    other = swap(same, "c")
    entering = plain(scan_kernel, (same,), [vmem], shape(HD, HD), vmem)
    carried = lax.all_gather(entering, "c")
    queries = plain(
        query_kernel,
        (inside, step_decay, state_readout, carried, both, norm_gain.reshape(1, 2 * HD)),
        [vmem, vmem, hbm, vmem, vmem, vmem],
        shape(2 * TOKENS, HD, dtype=bf16),
        vmem,
        [pltpu.VMEM((TOKENS, HD), bf16), pltpu.SemaphoreType.DMA],
    )

    attended = plain(
        attend_kernel,
        (queries, same, other),
        [vmem] * 3,
        shape(4, TOKENS // 2, 2 * HD, dtype=bf16),
        vmem,
        [pltpu.VMEM((CHIPS, 2 * TOKENS, 2 * SPAN), f32)] + [pltpu.VMEM((2 * TOKENS, HD), f32)] * 3,
        room=24,
    )
    attended, second = lax.optimization_barrier((attended, second))
    received = (first, second, third)
    swapped = swapped + [swap(part, "c") for part in (second, third)]
    attended = lax.all_to_all(attended, NEAR, 0, 0, tiled=True)
    vmem = pl.BlockSpec(memory_space=pltpu.VMEM)
    keep, send = plain(
        project_kernel,
        (attended, own_columns, *received, *swapped),
        [vmem] * 8,
        (shape(64, 2 * width, dtype=bf16),) * 2,
        (vmem,) * 2,
    )
    simple = functools.partial(pl.pallas_call, compiler_params=pltpu.CompilerParams(vmem_limit_bytes=40 * 1024 * 1024))
    partial = simple(add_kernel, out_shape=shape(64, 2 * width, dtype=bf16))(keep, swap(send, "yl"))
    parts = lax.all_to_all(partial.reshape(8, 8, 2 * width), OWNERS, 0, 0, tiled=True)
    return simple(finish_kernel, out_shape=shape(8, 4 * width, dtype=bf16))(parts)


def solution(mesh):
    fine = Mesh(mesh.devices.reshape(SIZES), AXES)
    placed = (
        P(PIPE, TENSOR),
        P(TENSOR, PIPE),
        P(None, PIPE, None),
        P(None, PIPE, None),
        P(TENSOR),
        P(TENSOR),
        P(None, PIPE, None),
        P(None, PIPE, None),
        P(None, PIPE, None),
        P(None, PIPE, None),
        P(PIPE),
        P(TENSOR, None),
    )
    return jax.shard_map(
        per_device,
        mesh=fine,
        in_specs=placed,
        out_specs=P(PIPE + TENSOR, None),
        check_vma=False,
    )
```

```python
import functools
import math

import jax
import jax.numpy as jnp
from jax import lax
from jax.experimental import pallas as pl
from jax.experimental.pallas import tpu as pltpu
from jax.sharding import Mesh
from jax.sharding import PartitionSpec as P

CACHE = 128
MH = 128
P_SIZE = 64
HD = 128
TOKENS = 256
SPAN = CACHE + TOKENS
TILE = 2 * HD + 16
HEAD = TILE + 16
ROWS = HEAD + 2 * SPAN
CHIPS = 8
HIDDEN = -1e30
SCALE = HD ** (-0.5) * math.log2(math.e)

AXES = ("x", "yh", "c", "yl", "za", "z1", "z0")
SIZES = (4, 2, 2, 2, 4, 2, 2)
PIPE = ("x", "yh", "c")
TENSOR = ("yl", "za", "z1", "z0")
CHIP = ("x", "yh")
BLOCKS = ("yh", "x")
NEAR = ("z1", "z0")
OWNERS = ("z1", "za")

bf16 = jnp.bfloat16
f32 = jnp.float32


def dot(a, b, contract=((1,), (0,))):
    return lax.dot_general(a, b, (contract, ((), ())), preferred_element_type=f32)


def thirds(value):
    high = value.astype(bf16)
    rest = value - high.astype(f32)
    middle = rest.astype(bf16)
    low = (rest - middle.astype(f32)).astype(bf16)
    return (low, middle, high)


def tri(transposed):
    first = lax.broadcasted_iota(jnp.int32, (TOKENS, TOKENS), 0)
    second = lax.broadcasted_iota(jnp.int32, (TOKENS, TOKENS), 1)
    return (first <= second) if transposed else (first >= second)


def cum_columns(decay):
    lower = tri(False).astype(f32).astype(bf16)
    return sum(dot(lower, part, ((1,), (1,))) for part in thirds(decay))


def cum_rows(decay):
    upper = tri(True).astype(f32).astype(bf16)
    return sum(dot(part, upper) for part in thirds(decay))


def low_lanes(rows):
    return lax.broadcasted_iota(jnp.int32, (rows, 2 * P_SIZE), 1) < P_SIZE


def spread(columns, half, rows):
    left, right = columns[:, 2 * half : 2 * half + 1], columns[:, 2 * half + 1 : 2 * half + 2]
    return jnp.where(low_lanes(rows), left, right)


def own_group():
    return lax.axis_index(("yl", "za"))


def state_kernel(x_ref, decay_ref, b_hbm, out_ref, b_ref, sem):
    copy = pltpu.make_async_copy(b_hbm.at[own_group()], b_ref, sem)
    copy.start()
    cum = cum_columns(decay_ref[...])
    last = cum[TOKENS - 1 :, :]
    tail = jnp.exp(last - cum)
    total = jnp.exp(-last)
    copy.wait()
    for half in range(2):
        inputs = x_ref[:, half * HD : (half + 1) * HD].astype(f32)
        weighted = (spread(tail, half, TOKENS) * inputs).astype(bf16)
        out_ref[half, 0:HD, :] = dot(b_ref[...], weighted, ((0,), (0,)))
        out_ref[half, HD : HD + 8, :] = spread(jnp.broadcast_to(total, (8, 4)), half, 8)


def block_of(chip):
    return 4 * (chip % 2) + chip // 2


def spread_copies(held, out_ref, begin, sems):
    rows = held.shape[0]
    copies = [pltpu.make_async_copy(held, out_ref.at[k, begin : begin + rows], sems.at[k]) for k in range(CHIPS)]
    for copy in copies:
        copy.start()
    for copy in copies:
        copy.wait()


def block_of(chip):
    return 4 * (chip % 2) + chip // 2


def spread_copies(held, out_ref, begin, sems):
    rows = held.shape[0]
    copies = [pltpu.make_async_copy(held, out_ref.at[k, begin : begin + rows], sems.at[k]) for k in range(CHIPS)]
    for copy in copies:
        copy.start()
    return copies


def fill_kernel(ck_ref, nk_ref, cv_ref, nv_ref, w_ref, len_hbm, out_ref, *refs):
    w_outs, (held, w_held, len_ref, in_sems, w_sems, sems) = refs[:2], refs[2:]
    core, side, group = lax.axis_index("c"), lax.axis_index("z1"), own_group()
    width = w_held.shape[2]
    loads, begin = [], HEAD - TILE
    for i, ref in enumerate((ck_ref, nk_ref, cv_ref, nv_ref)):
        rows = ref.shape[1]
        loads.append(pltpu.make_async_copy(ref.at[group], held.at[begin : begin + rows], in_sems.at[i]))
        begin = begin + rows
    pieces = []
    for i, half in enumerate((side, 1 - side)):
        columns = pl.ds(pl.multiple_of((2 * half + core) * width, width), width)
        pieces.append(pltpu.make_async_copy(w_ref.at[:, columns], w_held.at[i], in_sems.at[4 + i]))
    loads.append(pltpu.make_async_copy(len_hbm, len_ref, in_sems.at[6]))
    for copy in loads + pieces:
        copy.start()
    loads.pop().wait()
    slots = lax.broadcasted_iota(jnp.int32, (HEAD - TILE, HD), 1)
    held[0 : HEAD - TILE, :] = jnp.where(slots < len_ref[0], 0.0, HIDDEN).astype(bf16)
    for copy in loads:
        copy.wait()
    copies = spread_copies(held, out_ref, TILE, sems)
    for i, copy in enumerate(pieces):
        copy.wait()
        copies.append(pltpu.make_async_copy(w_held.at[i], w_outs[i], w_sems.at[i]))
        copies[-1].start()
    for copy in copies:
        copy.wait()


def pack_kernel(both_ref, filled_ref, out_ref, held, sems):
    core = lax.axis_index("c")
    first, second = both_ref[0, core], both_ref[1, core]
    state = first[0:HD] * second[HD : HD + 1] + second[0:HD]
    high = state.astype(bf16)
    held[0:HD, :] = high
    held[HD : 2 * HD, :] = (state - high.astype(f32)).astype(bf16)
    row = lax.broadcasted_iota(jnp.int32, (TILE - 2 * HD, HD), 0)
    tile = jnp.zeros((TILE - 2 * HD, HD), f32)
    for i, part in enumerate(thirds(first[HD : HD + 1] * second[HD : HD + 1])):
        tile = jnp.where(row == i, part.astype(f32), tile)
    held[2 * HD : TILE, :] = tile.astype(bf16)
    for copy in spread_copies(held, out_ref, 0, sems):
        copy.wait()


def scan_kernel(all_ref, out_ref):
    chip = lax.axis_index(CHIP)
    state = jnp.zeros((HD, HD), f32)
    for k in range(CHIPS - 1):
        block = block_of(k)
        tile = all_ref[block, 2 * HD : TILE, :].astype(f32)
        decay = tile[0:1] + tile[1:2] + tile[2:3]
        here = all_ref[block, 0:HD, :].astype(f32) + all_ref[block, HD : 2 * HD, :].astype(f32)
        state = jnp.where(k < chip, decay * state + here, state)
    out_ref[...] = state


def inside_kernel(group_ref, x_ref, decay_ref, b_ref, c_ref, gain_ref, y_ref):
    decay = decay_ref[...]
    columns, rows = cum_columns(decay), cum_rows(decay)
    causal = tri(False)
    gram = dot(c_ref[0], b_ref[0], ((1,), (1,)))
    for half in range(2):
        inputs = x_ref[:, half * HD : (half + 1) * HD]
        pieces = []
        for head in (2 * half, 2 * half + 1):
            diff = jnp.where(causal, columns[:, head : head + 1] - rows[head : head + 1, :], 0.0)
            weights = jnp.where(causal, gram * jnp.exp(-diff), 0.0).astype(bf16)
            pieces.append(dot(weights, inputs))
        low = low_lanes(TOKENS)
        skip = jnp.where(low_lanes(1), gain_ref[2 * half], gain_ref[2 * half + 1])
        y_ref[half] = jnp.where(low, pieces[0], pieces[1]) + skip * inputs.astype(f32)


def query_kernel(y_ref, decay_ref, c_hbm, carried_ref, both_ref, gain_ref, out_ref, c_ref, sem):
    core = lax.axis_index("c")
    copy = pltpu.make_async_copy(c_hbm.at[own_group()], c_ref, sem)
    copy.start()
    low = low_lanes(TOKENS)
    fade = jnp.exp(-cum_columns(decay_ref[...]))
    copy.wait()
    readout = c_ref[...]
    for half in range(2):
        carried = carried_ref[half]
        after = both_ref[0, half, HD : HD + 1] * carried + both_ref[0, half, 0:HD]
        carried = jnp.where(core == 1, after, carried)
        from_state = sum(dot(readout, part) for part in thirds(carried))
        y = y_ref[half] + spread(fade, half, TOKENS) * from_state
        square = y * y
        left = jnp.sum(jnp.where(low, square, 0.0), axis=1, keepdims=True)
        right = jnp.sum(jnp.where(low, 0.0, square), axis=1, keepdims=True)
        mean = jnp.where(low, left, right) * (1.0 / P_SIZE)
        normed = y * lax.rsqrt(mean + 1e-05) * gain_ref[0:1, half * HD : (half + 1) * HD]
        out_ref[half * TOKENS : (half + 1) * TOKENS, :] = normed.astype(bf16)


def attend_kernel(q_ref, a_ref, b_ref, out_ref, scores_ref, top_ref, sum_ref, acc_ref):
    chip, core = lax.axis_index(CHIP), lax.axis_index("c")
    count = q_ref.shape[0]
    sides = (a_ref, b_ref)
    top_ref[...] = jnp.full((count, HD), -jnp.inf, f32)

    def score(k, side, extra, causal):
        bias = sides[side][block_of(k), TILE:HEAD, :].astype(f32)[0:1]
        raw = dot(q_ref[...], sides[side][block_of(k), HEAD : HEAD + SPAN, :], ((1,), (1,))) * SCALE
        top = top_ref[...]
        for tile in range(SPAN // HD):
            part = raw[:, tile * HD : (tile + 1) * HD]
            if tile == 0:
                part = part + (bias if extra is None else bias + extra)
            elif causal:
                token = lax.broadcasted_iota(jnp.int32, (count, HD), 0) % TOKENS
                key = lax.broadcasted_iota(jnp.int32, (count, HD), 1) + (tile - 1) * HD
                part = jnp.where(key <= token, part, HIDDEN)
            elif extra is not None:
                part = part + extra
            top = jnp.maximum(top, part)
            scores_ref[k, :, side * SPAN + tile * HD : side * SPAN + (tile + 1) * HD] = part
        top_ref[...] = top

    def early(k, carry):
        score(k, 0, None, False)
        score(k, 1, None, False)
        return carry

    lax.fori_loop(0, chip, early, 0)
    score(chip, 0, None, True)
    score(chip, 1, jnp.where(core == 1, 0.0, HIDDEN), False)

    top = jnp.max(top_ref[...], axis=1, keepdims=True)
    top_ref[...] = jnp.broadcast_to(top, (count, HD))
    sum_ref[...] = jnp.zeros((count, HD), f32)
    acc_ref[...] = jnp.zeros((count, HD), f32)

    def late(k, carry):
        top = top_ref[...]
        total = sum_ref[...]
        acc = acc_ref[...]
        for side in range(2):
            probs = []
            for tile in range(SPAN // HD):
                part = scores_ref[k, :, side * SPAN + tile * HD : side * SPAN + (tile + 1) * HD]
                expo = jnp.exp2(part - top)
                total = total + expo
                probs.append(expo.astype(bf16))
            acc = acc + dot(jnp.concatenate(probs, axis=1), sides[side][block_of(k), HEAD + SPAN :, :])
        sum_ref[...] = total
        acc_ref[...] = acc
        return carry

    lax.fori_loop(0, chip + 1, late, 0)
    total = jnp.sum(sum_ref[...], axis=1, keepdims=True)
    result = acc_ref[...] / total
    for z0 in range(2):
        for half in range(2):
            blocks = [16 * yl + 4 * za + 2 * z1 + z0 for yl in range(2) for z1 in range(2) for za in range(4)]
            rows = [half * TOKENS + 8 * block for block in blocks]
            piece = jnp.concatenate([result[row : row + 8] for row in rows], axis=0).astype(bf16)
            for z1 in range(2):
                out_ref[2 * z1 + z0, :, half * HD : (half + 1) * HD] = piece


def project_kernel(att_ref, own_ref, r1, r2, r3, s1, s2, s3, keep_ref, send_ref):
    near, core, side = lax.axis_index(NEAR), lax.axis_index("c"), lax.axis_index("yl")
    rows, width = keep_ref.shape[0], r1.shape[1]

    def run(others, begin):
        total = dot(att_ref[near], own_ref[:, begin : begin + width])
        for i, ref in enumerate(others):
            total = total + dot(att_ref[near ^ (i + 1)], ref[...])
        total = total.astype(bf16)

        @pl.when(side == 0)
        def _():
            keep_ref[:, begin : begin + width] = total[:rows]
            send_ref[:, begin : begin + width] = total[rows:]

        @pl.when(side == 1)
        def _():
            keep_ref[:, begin : begin + width] = total[rows:]
            send_ref[:, begin : begin + width] = total[:rows]

    @pl.when(core == 0)
    def _():
        run((r1, r2, r3), 0)
        run((s1, s2, s3), width)

    @pl.when(core == 1)
    def _():
        run((s1, s2, s3), 0)
        run((r1, r2, r3), width)


def add_kernel(first_ref, second_ref, out_ref):
    out_ref[...] = (first_ref[...].astype(f32) + second_ref[...].astype(f32)).astype(bf16)


def finish_kernel(parts_ref, out_ref):
    for half in range(2):
        total = parts_ref[4 * half].astype(f32)
        for i in range(1, 4):
            total = total + parts_ref[4 * half + i].astype(f32)
        width = parts_ref.shape[2]
        out_ref[:, half * width : (half + 1) * width] = total.astype(bf16)


def whole(shape):
    return pl.BlockSpec(shape, lambda *_: (0,) * len(shape))


SMEM = pl.BlockSpec(memory_space=pltpu.SMEM)


def call(kernel, scalars, args, in_specs, out_shape, out_specs, grid=(1,), scratch=(), room=16, aliases=None):
    return pl.pallas_call(
        kernel,
        out_shape=out_shape,
        grid_spec=pltpu.PrefetchScalarGridSpec(
            num_scalar_prefetch=1, grid=grid, in_specs=in_specs, out_specs=out_specs, scratch_shapes=scratch
        ),
        input_output_aliases=aliases or {},
        compiler_params=pltpu.CompilerParams(vmem_limit_bytes=room * 1024 * 1024),
        cost_estimate=pl.CostEstimate(flops=0, bytes_accessed=1 << 12, transcendentals=0),
    )(scalars, *args)


def plain(kernel, args, in_specs, out_shape, out_specs, scratch=(), aliases=None, room=16):
    return pl.pallas_call(
        kernel,
        out_shape=out_shape,
        in_specs=in_specs,
        out_specs=out_specs,
        scratch_shapes=scratch,
        input_output_aliases=aliases or {},
        compiler_params=pltpu.CompilerParams(vmem_limit_bytes=room * 1024 * 1024),
        cost_estimate=pl.CostEstimate(flops=0, bytes_accessed=1 << 12, transcendentals=0),
    )(*args)


def shape(*dims, dtype=f32):
    return jax.ShapeDtypeStruct(dims, dtype)


def swap(array, axis):
    return lax.ppermute(array, axis, [(0, 1), (1, 0)])


def flip(array, i):
    return lax.ppermute(array, NEAR, [(j, j ^ i) for j in range(4)])


def per_device(
    ssm_inputs,
    step_decay,
    state_inputs,
    state_readout,
    skip_gain,
    norm_gain,
    new_keys,
    new_values,
    cache_keys,
    cache_values,
    cache_len,
    out_weight,
):
    width = out_weight.shape[1] // 4
    core = lax.axis_index("c")
    near = lax.axis_index(NEAR)
    group = lax.axis_index(("yl", "za")).astype(jnp.int32)
    of_group = lambda rows: pl.BlockSpec((1, rows, HD), lambda i, s: (s[3], 0, 0))

    hbm = pl.BlockSpec(memory_space=pltpu.HBM)
    vmem = pl.BlockSpec(memory_space=pltpu.VMEM)
    filled, first, second = plain(
        fill_kernel,
        (cache_keys, new_keys, cache_values, new_values, out_weight, cache_len),
        [hbm] * 6,
        (shape(CHIPS, ROWS, HD, dtype=bf16),) + (shape(2 * HD, width, dtype=bf16),) * 2,
        (hbm,) * 3,
        [
            pltpu.VMEM((ROWS - TILE, HD), bf16),
            pltpu.VMEM((2, 2 * HD, width), bf16),
            pltpu.SMEM((1,), jnp.int32),
            pltpu.SemaphoreType.DMA((7,)),
            pltpu.SemaphoreType.DMA((2,)),
            pltpu.SemaphoreType.DMA((CHIPS,)),
        ],
        room=60,
    )
    step_decay, filled = lax.optimization_barrier((step_decay, filled))

    own = plain(
        state_kernel,
        (ssm_inputs, step_decay, state_inputs),
        [vmem, vmem, hbm],
        shape(2, HD + 8, HD),
        vmem,
        [pltpu.VMEM((TOKENS, HD), bf16), pltpu.SemaphoreType.DMA],
    )
    both = lax.all_gather(own, "c")
    packed = plain(
        pack_kernel,
        (both, filled),
        [vmem, hbm],
        shape(CHIPS, ROWS, HD, dtype=bf16),
        hbm,
        [pltpu.VMEM((TILE, HD), bf16), pltpu.SemaphoreType.DMA((CHIPS,))],
        {1: 0},
        room=60,
    )
    place = jnp.stack([lax.axis_index(CHIP), core, near, group]).astype(jnp.int32)
    second = flip(second, 2)
    third = flip(second, 1)
    same = lax.all_to_all(packed, BLOCKS, 0, 0, tiled=True)
    inside = call(
        inside_kernel,
        place,
        (ssm_inputs, step_decay, state_inputs, state_readout, skip_gain),
        [whole((TOKENS, 2 * HD)), whole((4, TOKENS)), of_group(TOKENS), of_group(TOKENS), SMEM],
        shape(2, TOKENS, HD),
        whole((2, TOKENS, HD)),
    )
    first = flip(first, 1)
    own_columns = lax.dynamic_slice_in_dim(out_weight, 2 * (near // 2) * width, 2 * width, 1)
    first, inside = lax.optimization_barrier((first, inside))
    swapped = [swap(first, "c")]
    same, second, swapped, own_columns = lax.optimization_barrier((same, second, swapped, own_columns))
    other = swap(same, "c")
    entering = plain(scan_kernel, (same,), [vmem], shape(HD, HD), vmem)
    carried = lax.all_gather(entering, "c")
    queries = plain(
        query_kernel,
        (inside, step_decay, state_readout, carried, both, norm_gain.reshape(1, 2 * HD)),
        [vmem, vmem, hbm, vmem, vmem, vmem],
        shape(2 * TOKENS, HD, dtype=bf16),
        vmem,
        [pltpu.VMEM((TOKENS, HD), bf16), pltpu.SemaphoreType.DMA],
    )

    attended = plain(
        attend_kernel,
        (queries, same, other),
        [vmem] * 3,
        shape(4, TOKENS // 2, 2 * HD, dtype=bf16),
        vmem,
        [pltpu.VMEM((CHIPS, 2 * TOKENS, 2 * SPAN), f32)] + [pltpu.VMEM((2 * TOKENS, HD), f32)] * 3,
        room=24,
    )
    attended, second = lax.optimization_barrier((attended, second))
    received = (first, second, third)
    swapped = swapped + [swap(part, "c") for part in (second, third)]
    attended = lax.all_to_all(attended, NEAR, 0, 0, tiled=True)
    vmem = pl.BlockSpec(memory_space=pltpu.VMEM)
    keep, send = plain(
        project_kernel,
        (attended, own_columns, *received, *swapped),
        [vmem] * 8,
        (shape(64, 2 * width, dtype=bf16),) * 2,
        (vmem,) * 2,
    )
    simple = functools.partial(pl.pallas_call, compiler_params=pltpu.CompilerParams(vmem_limit_bytes=40 * 1024 * 1024))
    partial = simple(add_kernel, out_shape=shape(64, 2 * width, dtype=bf16))(keep, swap(send, "yl"))
    parts = lax.all_to_all(partial.reshape(8, 8, 2 * width), OWNERS, 0, 0, tiled=True)
    return simple(finish_kernel, out_shape=shape(8, 4 * width, dtype=bf16))(parts)


def solution(mesh):
    fine = Mesh(mesh.devices.reshape(SIZES), AXES)
    placed = (
        P(PIPE, TENSOR),
        P(TENSOR, PIPE),
        P(None, PIPE, None),
        P(None, PIPE, None),
        P(TENSOR),
        P(TENSOR),
        P(None, PIPE, None),
        P(None, PIPE, None),
        P(None, PIPE, None),
        P(None, PIPE, None),
        P(PIPE),
        P(TENSOR, None),
    )
    return jax.shard_map(
        per_device,
        mesh=fine,
        in_specs=placed,
        out_specs=P(PIPE + TENSOR, None),
        check_vma=False,
    )
```
